256 devices in a mesh: row: 32 (over z, x_hi, core), col: 8 (over y, x_lo).
Axes of the slice: x: 4 (x_hi: 2, x_lo: 2; x = x_hi * 2 + x_lo), y: 4, z: 8, core: 2. Of those that a mesh axis runs over, the one named last changes fastest.
Arguments:
- pair_map: bfloat16 [64, 1024, 1024], P(None, 'row', 'col'), may hold values from -6 to 6
- kernel_one_a: bfloat16 [3, 3, 64, 64], replicated, may hold values from -0.25 to 0.25
- bias_one_a: float32 [64], replicated, may hold values from -3 to 3
- kernel_one_b: bfloat16 [3, 3, 64, 64], replicated, may hold values from -0.25 to 0.25
- bias_one_b: float32 [64], replicated, may hold values from -3 to 3
- kernel_two_a: bfloat16 [3, 3, 64, 64], replicated, may hold values from -0.25 to 0.25
- bias_two_a: float32 [64], replicated, may hold values from -3 to 3
- kernel_two_b: bfloat16 [3, 3, 64, 64], replicated, may hold values from -0.25 to 0.25
- bias_two_b: float32 [64], replicated, may hold values from -3 to 3
Outputs:
- pair_out: bfloat16 [64, 1024, 1024], P(None, 'row', 'col')
The draws below stay inside these ranges and needn't reach their ends.
All inputs are finite; a program needn't handle non-finite values.
Results may differ from the reference program's by a relative error of at most 0.0064.
Values may be sent and summed in bfloat16 or wider, within the bound.
A program may use at most 64 MiB of HBM per device.

```python
import jax
import jax.numpy as jnp
from jax import lax

CHAN = 64
RESIDUES = 1024


def block_scale(key, dims, shards, low, largest):
    def one(axis_at, parts):
        heights = jax.random.uniform(jax.random.fold_in(jax.random.fold_in(key, 6), axis_at), (parts,), jnp.float32, low / len(shards), largest / len(shards))
        return jnp.repeat(jnp.exp(heights), dims[axis_at] // parts).reshape((-1,) + (1,) * (len(dims) - axis_at - 1))

    level = one(*shards[0])
    for cut in shards[1:]:
        level = level * one(*cut)
    return level


def scatter_about(key, extent, spread, most, cuts=(), held_as=jnp.bfloat16):
    values = spread * jax.random.normal(key, extent, jnp.float32)
    if cuts:
        values = values * block_scale(key, extent, cuts, -0.22, 0.18)
    return jnp.clip(values, -most, most).astype(held_as)


def setup_inputs(seed: int = 0) -> dict:
    arg_keys = jax.random.split(jax.random.key(seed), 10)
    pair_map = scatter_about(arg_keys[0], (CHAN, RESIDUES, RESIDUES), 1.0, 6.0, ((1, 32), (2, 8)))
    kernel_one_a = scatter_about(arg_keys[1], (3, 3, CHAN, CHAN), (9 * CHAN) ** -0.5, 0.25)
    bias_one_a = scatter_about(arg_keys[2], (CHAN,), 0.5, 3.0, (), jnp.float32)
    kernel_one_b = scatter_about(arg_keys[3], (3, 3, CHAN, CHAN), (9 * CHAN) ** -0.5, 0.25)
    bias_one_b = scatter_about(arg_keys[4], (CHAN,), 0.5, 3.0, (), jnp.float32)
    kernel_two_a = scatter_about(arg_keys[5], (3, 3, CHAN, CHAN), (9 * CHAN) ** -0.5, 0.25)
    bias_two_a = scatter_about(arg_keys[6], (CHAN,), 0.5, 3.0, (), jnp.float32)
    kernel_two_b = scatter_about(arg_keys[7], (3, 3, CHAN, CHAN), (9 * CHAN) ** -0.5, 0.25)
    bias_two_b = scatter_about(arg_keys[8], (CHAN,), 0.5, 3.0, (), jnp.float32)
    return {"pair_map": pair_map, "kernel_one_a": kernel_one_a, "bias_one_a": bias_one_a, "kernel_one_b": kernel_one_b, "bias_one_b": bias_one_b, "kernel_two_a": kernel_two_a, "bias_two_a": bias_two_a, "kernel_two_b": kernel_two_b, "bias_two_b": bias_two_b}


def apply_dilated_conv(pair_field, filter_weight, dilation_rate):
    return lax.conv_general_dilated(pair_field[None], filter_weight.astype(jnp.float32), window_strides=(1, 1), padding=((dilation_rate, dilation_rate), (dilation_rate, dilation_rate)), rhs_dilation=(dilation_rate, dilation_rate), dimension_numbers=("NCHW", "HWOI", "NCHW"), precision=lax.Precision.HIGHEST)[0]


def residual_block(source_map, first_filter, first_bias, second_filter, second_bias, dilation_rate):
    wide_features = source_map.astype(jnp.float32)
    hidden_features = jax.nn.elu(apply_dilated_conv(wide_features, first_filter, dilation_rate) + first_bias[:, None, None]).astype(jnp.bfloat16)
    hidden_features = lax.optimization_barrier(hidden_features).astype(jnp.float32)
    block_output = jax.nn.elu(wide_features + apply_dilated_conv(hidden_features, second_filter, dilation_rate) + second_bias[:, None, None]).astype(jnp.bfloat16)
    block_output = lax.optimization_barrier(block_output).astype(jnp.float32)
    return ((block_output + jnp.transpose(block_output, (0, 2, 1))) * 0.5).astype(jnp.bfloat16)


def reference(pair_map, kernel_one_a, bias_one_a, kernel_one_b, bias_one_b, kernel_two_a, bias_two_a, kernel_two_b, bias_two_b):
    first = residual_block(pair_map, kernel_one_a, bias_one_a, kernel_one_b, bias_one_b, 2)
    return residual_block(first, kernel_two_a, bias_two_a, kernel_two_b, bias_two_b, 4)
```

```python
import functools

import jax
import jax.numpy as jnp
from jax import lax
from jax.experimental import pallas as pl
from jax.experimental.pallas import tpu as pltpu
from jax.sharding import PartitionSpec as P

MESH = pl.DeviceIdType.MESH
F32, BF16 = jnp.float32, jnp.bfloat16
NT = (((1,), (1,)), ((), ()))
ROWS, COLS, CHAN, SIDE, QUAD = 32, 128, 64, 8, 4
ROW_PAD, COL_PAD, HID_ROW, HID_COL = 8, 16, 4, 8
NEIGHBOURS = [(dr, dc) for dr in (-1, 0, 1) for dc in (-1, 0, 1) if dr or dc]


def elu(v):
    return jnp.where(v > 0, v, jnp.exp(jnp.minimum(v, 0.0)) - 1.0)


def rounded(v):
    return v.astype(BF16).astype(F32)


def low_lanes(shape):
    return lax.broadcasted_iota(jnp.int32, shape, len(shape) - 1) < CHAN


def doubled(packed):
    turned = pltpu.roll(packed, CHAN, packed.ndim - 1)
    low = low_lanes(packed.shape)
    return jnp.where(low, packed, turned), jnp.where(low, turned, packed)


def paired(first, second):
    return jnp.where(low_lanes(first.shape), first, second)


class Halo:
    def __init__(self, rows, frame, send, recv, send_sem, recv_sem, row, col):
        self.rows, self.frame = rows, frame
        self.send, self.recv = send, recv
        self.send_sem, self.recv_sem = send_sem, recv_sem
        self.row, self.col = row, col

    def parts(self, at):
        dr, dc = NEIGHBOURS[at]
        if dc == 0:
            return 0 if dr < 0 else 1, self.rows * 4
        if dr == 0:
            return 2 if dc < 0 else 3, 8
        return 4 + (dr > 0) * 2 + (dc > 0), self.rows // 4

    def copy(self, at):
        dr, dc = NEIGHBOURS[at]
        there = len(NEIGHBOURS) - 1 - at
        mine, count = self.parts(at)
        other, _ = self.parts(there)
        device = (lax.rem(self.row + dr + 32, 32), lax.rem(self.col + dc + SIDE, SIDE))
        return pltpu.make_async_remote_copy(
            self.send.at[mine, pl.ds(0, count)],
            self.recv.at[other, pl.ds(0, count)],
            self.send_sem.at[mine],
            self.recv_sem.at[other],
            device_id=device,
            device_id_type=MESH,
        )

    def incoming(self, at):
        mine, count = self.parts(at)
        there = self.recv.at[mine, pl.ds(0, count)]
        return pltpu.make_async_copy(there, there, self.recv_sem.at[mine])

    def start(self):
        frame, rows = self.frame, self.rows
        for at, (dr, dc) in enumerate(NEIGHBOURS):
            mine, _ = self.parts(at)
            top = ROW_PAD if dr < 0 else ROW_PAD + ROWS - rows
            left = COL_PAD if dc < 0 else COL_PAD + COLS - 8
            if dc == 0:

                def pack_row(i, _, mine=mine, top=top):
                    line = frame[top + i, COL_PAD : COL_PAD + COLS, :]
                    both = paired(line[:64], line[64:]).astype(BF16)
                    self.send[mine, pl.ds(i * 4, 4)] = both.reshape(4, 16, 128)
                    return 0

                lax.fori_loop(0, rows, pack_row, 0)
            else:
                base, many = (ROW_PAD, ROWS // 4) if dr == 0 else (top, rows // 4)

                def pack_block(t, _, mine=mine, left=left, base=base):
                    block = frame[pl.ds(base + 4 * t, 4), left : left + 8, :]
                    both = paired(block[:2].reshape(16, 128), block[2:].reshape(16, 128))
                    self.send[mine, t] = both.astype(BF16)
                    return 0

                lax.fori_loop(0, many, pack_block, 0)
            self.copy(at).start()

    def finish(self):
        frame, rows = self.frame, self.rows
        for at, (dr, dc) in enumerate(NEIGHBOURS):
            self.incoming(at).wait()
            mine, _ = self.parts(at)
            inside = jnp.logical_and(
                jnp.logical_and(self.row + dr >= 0, self.row + dr < 32),
                jnp.logical_and(self.col + dc >= 0, self.col + dc < SIDE),
            )
            top = ROW_PAD - rows if dr < 0 else ROW_PAD + ROWS
            left = COL_PAD - 8 if dc < 0 else COL_PAD + COLS
            if dc == 0:

                def place_row(i, _, mine=mine, top=top, inside=inside):
                    line = self.recv[mine, pl.ds(i * 4, 4)].reshape(64, 128).astype(F32)
                    first, second = doubled(jnp.where(inside, line, 0.0))
                    frame[top + i, COL_PAD : COL_PAD + 64, :] = first
                    frame[top + i, COL_PAD + 64 : COL_PAD + 128, :] = second
                    return 0

                lax.fori_loop(0, rows, place_row, 0)
            else:
                base, many = (ROW_PAD, ROWS // 4) if dr == 0 else (top, rows // 4)

                def place_block(t, _, mine=mine, left=left, base=base, inside=inside):
                    block = self.recv[mine, t].astype(F32)
                    first, second = doubled(jnp.where(inside, block, 0.0))
                    frame[pl.ds(base + 4 * t, 2), left : left + 8, :] = first.reshape(2, 8, 128)
                    frame[pl.ds(base + 4 * t + 2, 2), left : left + 8, :] = second.reshape(2, 8, 128)
                    return 0

                lax.fori_loop(0, many, place_block, 0)
        for at in range(len(NEIGHBOURS)):
            self.copy(at).wait_send()


def three_taps(kernel, ky, swapped=False):
    pick = lambda kx: kernel[kx, ky] if swapped else kernel[ky, kx]
    zeros = jnp.zeros((CHAN, CHAN), BF16)
    return jnp.concatenate([pick(0), pick(1), pick(2), zeros], axis=1)


def body(
    x_ref, k1a, b1a, k1b, b1b, k2a, b2a, k2b, b2b, out_ref,
    flat, frame, slab, hidden, wide, block_y, outbox, transit, inbox,
    halo_send, halo_recv, w1a, w1b, w2a, w2b,
    halo_ss, halo_rs, ss1, rs1, ss2, rs2,
):
    row, col = lax.axis_index("row"), lax.axis_index("col")
    z, quarter = row // QUAD, lax.rem(row, QUAD)

    barrier = pltpu.get_barrier_semaphore()

    def greet(device):
        pl.semaphore_signal(barrier, inc=1, device_id=device, device_id_type=MESH)

    for dr, dc in NEIGHBOURS:
        greet((lax.rem(row + dr + 32, 32), lax.rem(col + dc + SIDE, SIDE)))

    def greet_plane(t, _):
        other = lax.rem(col + t, SIDE)
        for k in range(QUAD):

            @pl.when(jnp.logical_or(t > 0, quarter != k))
            def _():
                greet((z * QUAD + k, other))

        @pl.when(jnp.logical_or(col != z, t > 0))
        def _():
            greet((col * QUAD + quarter, other))

        return 0

    lax.fori_loop(0, SIDE, greet_plane, 0)
    waits = 8 + 31 + SIDE - jnp.where(col == z, 1, 0)

    def widen(g, _):
        flat[pl.ds(g * 256, 256), :] = x_ref[pl.ds(g * 8, 8)].astype(F32).reshape(256, 128)
        return 0

    lax.fori_loop(0, CHAN // 8, widen, 0)
    same = lax.broadcasted_iota(jnp.int32, (COLS, COLS), 0) == lax.broadcasted_iota(
        jnp.int32, (COLS, COLS), 1
    )
    unit = same.astype(F32).astype(BF16)

    def turn(i, _):
        line = flat[pl.ds(i, CHAN, stride=ROWS), :].astype(BF16)
        both = jnp.concatenate([line, line], axis=0)
        frame[ROW_PAD + i, COL_PAD : COL_PAD + COLS, :] = lax.dot_general(
            unit, both, NT, preferred_element_type=F32
        )
        return 0

    lax.fori_loop(0, ROWS, turn, 0)

    for ky in range(3):
        for target, kernel in ((w1a, k1a), (w1b, k1b)):
            taps = three_taps(kernel, ky)
            target[:, ky * 256 : ky * 256 + 256] = jnp.concatenate([taps, taps], axis=0)
        w2a[:, ky * 256 : ky * 256 + 256] = jnp.concatenate(
            [three_taps(k2a, ky), three_taps(k2a, ky, True)], axis=0
        )
        for kx in range(3):
            zeros = jnp.zeros((CHAN, CHAN), BF16)
            upper = jnp.concatenate([k2b[ky, kx], zeros], axis=1)
            lower = jnp.concatenate([zeros, k2b[kx, ky]], axis=1)
            at = ky * 384 + kx * 128
            w2b[:, at : at + 128] = jnp.concatenate([upper, lower], axis=0)

    def bias(ref):
        return jnp.concatenate([ref[...], ref[...]], axis=1)

    def within(first_row, count):
        shape = (count, 144, 128)
        i = lax.broadcasted_iota(jnp.int32, shape, 0) + (first_row + row * ROWS)
        j = lax.broadcasted_iota(jnp.int32, shape, 1) + (col * COLS - HID_COL)
        full = jnp.logical_and(i >= 0, i < 32 * ROWS)
        return jnp.logical_and(full, jnp.logical_and(j >= 0, j < SIDE * COLS))

    pl.semaphore_wait(barrier, waits)

    halo = Halo(4, frame, halo_send.at[0], halo_recv.at[0], halo_ss.at[0], halo_rs.at[0], row, col)
    halo.start()
    halo.finish()

    def shifted(d, top):
        def one(i, _):
            at = COL_PAD - HID_COL
            left = frame[top + i, at - d : at - d + 144, :]
            here = frame[top + i, at : at + 144, :]
            right = frame[top + i, at + d : at + d + 144, :]
            slab[top + i, :, 0:128] = paired(left, here).astype(BF16)
            slab[top + i, :, 128:256] = right.astype(BF16)
            return 0

        return one

    def conv_a(d, weights, bias_ref, step):
        def one(t, _):
            i = t * step - d
            lhs = jnp.concatenate(
                [
                    slab[pl.ds(i + ROW_PAD + (ky - 1) * d, step)].reshape(step * 144, 256)
                    for ky in range(3)
                ],
                axis=1,
            )
            total = lax.dot_general(lhs, weights[...], NT, preferred_element_type=F32)
            value = rounded(elu(total + bias(bias_ref))).reshape(step, 144, 128)
            hidden[pl.ds(i + HID_ROW, step)] = jnp.where(within(i, step), value, 0.0)
            return 0

        return one

    lax.fori_loop(0, 40, shifted(2, ROW_PAD - 4), 0)
    lax.fori_loop(0, 9, conv_a(2, w1a, b1a, 4), 0)

    def hidden_taps(i, _):
        at = i + HID_ROW - 2
        left = hidden[at, HID_COL - 2 : HID_COL + 126, :]
        here = hidden[at, HID_COL : HID_COL + 128, :]
        right = hidden[at, HID_COL + 2 : HID_COL + 130, :]
        slab[i, 0:128, 0:128] = paired(left, here).astype(BF16)
        slab[i, 0:128, 128:256] = right.astype(BF16)
        return 0

    lax.fori_loop(0, 36, hidden_taps, 0)

    def conv_b_one(t, _):
        i = t * 4
        lhs = jnp.concatenate(
            [slab[pl.ds(i + 2 * ky, 4), 0:128, :].reshape(512, 256) for ky in range(3)], axis=1
        )
        total = lax.dot_general(lhs, w1b[...], NT, preferred_element_type=F32)
        here = frame[pl.ds(ROW_PAD + i, 4), COL_PAD : COL_PAD + COLS, :].reshape(512, 128)
        block_y[pl.ds(i * COLS, 512), :] = rounded(elu(here + total + bias(b1b)))
        return 0

    lax.fori_loop(0, ROWS // 4, conv_b_one, 0)

    def spread(t, _):
        via = lax.rem(col + 1 + t, SIDE)
        for k in range(QUAD):
            for u in range(4):
                column = block_y[pl.ds(32 * k + 4 * via + u, ROWS, stride=COLS), :]
                outbox[via, k, u] = paired(column[:16], column[16:]).astype(BF16)
            alone = jnp.logical_and(t == SIDE - 1, quarter == k)

            @pl.when(alone)
            def _():
                pltpu.make_async_copy(
                    outbox.at[via, k], transit.at[col, quarter], rs1.at[col]
                ).start()

            @pl.when(jnp.logical_not(alone))
            def _():
                pltpu.make_async_remote_copy(
                    outbox.at[via, k],
                    transit.at[col, quarter],
                    ss1,
                    rs1.at[col],
                    device_id=(z * QUAD + k, via),
                    device_id_type=MESH,
                ).start()

        return 0

    lax.fori_loop(0, SIDE, spread, 0)

    def forward(t, _):
        origin = lax.rem(col + 2 * SIDE - 1 - t, SIDE)
        pltpu.make_async_copy(transit.at[origin], transit.at[origin], rs1.at[origin]).wait()
        alone = jnp.logical_and(origin == z, col == z)

        @pl.when(alone)
        def _():
            pltpu.make_async_copy(transit.at[origin], inbox.at[col], rs2.at[col]).start()

        @pl.when(jnp.logical_not(alone))
        def _():
            pltpu.make_async_remote_copy(
                transit.at[origin],
                inbox.at[col],
                ss2,
                rs2.at[col],
                device_id=(origin * QUAD + quarter, z),
                device_id_type=MESH,
            ).start()

        return 0

    lax.fori_loop(0, SIDE, forward, 0)

    def arrive(t, _):
        via = lax.rem(z + 1 + t, SIDE)
        pltpu.make_async_copy(inbox.at[via], inbox.at[via], rs2.at[via]).wait()
        for u in range(4):
            i = via * 4 + u
            for k in range(QUAD):
                mirror = doubled(inbox[via, k, u].astype(F32))
                for half in range(2):
                    j = 32 * k + 16 * half
                    own = block_y[pl.ds(pl.multiple_of(i * COLS + j, 16), 16), :]
                    frame[ROW_PAD + i, COL_PAD + j : COL_PAD + j + 16, :] = rounded(
                        (own + mirror[half]) * 0.5
                    )
        return 0

    lax.fori_loop(0, SIDE, arrive, 0)

    halo = Halo(8, frame, halo_send.at[1], halo_recv.at[1], halo_ss.at[1], halo_rs.at[1], row, col)
    halo.start()
    halo.finish()

    lax.fori_loop(0, 48, shifted(4, 0), 0)
    lax.fori_loop(0, 10, conv_a(4, w2a, b2a, 4), 0)

    def wide_taps(i, _):
        for kx in range(3):
            at = HID_COL + 4 * (kx - 1)
            wide[i, :, kx * 128 : kx * 128 + 128] = hidden[i, at : at + 128, :].astype(BF16)
        return 0

    lax.fori_loop(0, 40, wide_taps, 0)

    lane = lax.broadcasted_iota(jnp.int32, (CHAN, 128), 1)
    chan = lax.broadcasted_iota(jnp.int32, (CHAN, 128), 0)
    mean = jnp.where(jnp.logical_or(lane == chan, lane == chan + CHAN), 0.5, 0.0).astype(BF16)

    def conv_b_two(t, _):
        i = t * 4
        lhs = jnp.concatenate(
            [wide[pl.ds(i + 4 * ky, 4)].reshape(512, 384) for ky in range(3)], axis=1
        )
        total = lax.dot_general(lhs, w2b[...], NT, preferred_element_type=F32)
        here = frame[pl.ds(ROW_PAD + i, 4), COL_PAD : COL_PAD + COLS, :].reshape(512, 128)
        both = elu(here + total + bias(b2b)).astype(BF16)
        for u in range(4):
            line = both[u * COLS : (u + 1) * COLS]
            flat[pl.ds(i + u, CHAN, stride=ROWS), :] = lax.dot_general(
                mean, line, NT, preferred_element_type=F32
            )
        return 0

    lax.fori_loop(0, ROWS // 4, conv_b_two, 0)

    def narrow(g, _):
        out_ref[pl.ds(g * 8, 8)] = flat[pl.ds(g * 256, 256), :].reshape(8, ROWS, COLS).astype(BF16)
        return 0

    lax.fori_loop(0, CHAN // 8, narrow, 0)

    def sent_one(t, _):
        for k in range(QUAD):

            @pl.when(jnp.logical_not(jnp.logical_and(t == SIDE - 1, quarter == k)))
            def _():
                pltpu.make_async_copy(outbox.at[0, 0], outbox.at[0, 0], ss1).wait()

        @pl.when(jnp.logical_or(t > 0, col != z))
        def _():
            pltpu.make_async_copy(transit.at[0], transit.at[0], ss2).wait()

        return 0

    lax.fori_loop(0, SIDE, sent_one, 0)


def shards(pair_map, k1a, b1a, k1b, b1b, k2a, b2a, k2b, b2b):
    wide = lambda b: b.reshape(1, CHAN)
    vmem = pl.BlockSpec(memory_space=pltpu.VMEM)
    dma, regular = pltpu.SemaphoreType.DMA, pltpu.SemaphoreType.REGULAR
    return pl.pallas_call(
        body,
        out_shape=jax.ShapeDtypeStruct((CHAN, ROWS, COLS), BF16),
        in_specs=[vmem] * 9,
        out_specs=vmem,
        scratch_shapes=[
            pltpu.VMEM((CHAN * ROWS, COLS), F32),
            pltpu.VMEM((ROWS + 2 * ROW_PAD, COLS + 2 * COL_PAD, 128), F32),
            pltpu.VMEM((ROWS + 2 * ROW_PAD, 144, 256), BF16),
            pltpu.VMEM((ROWS + 2 * HID_ROW, 144, 128), F32),
            pltpu.VMEM((ROWS + 2 * HID_ROW, COLS, 384), BF16),
            pltpu.VMEM((ROWS * COLS, 128), F32),
            pltpu.VMEM((SIDE, QUAD, 4, 16, 128), BF16),
            pltpu.VMEM((SIDE, QUAD, 4, 16, 128), BF16),
            pltpu.VMEM((SIDE, QUAD, 4, 16, 128), BF16),
            pltpu.VMEM((2, 8, 32, 16, 128), BF16),
            pltpu.VMEM((2, 8, 32, 16, 128), BF16),
            pltpu.VMEM((128, 768), BF16),
            pltpu.VMEM((128, 768), BF16),
            pltpu.VMEM((128, 768), BF16),
            pltpu.VMEM((128, 1152), BF16),
            dma((2, 8)),
            dma((2, 8)),
            dma,
            dma((SIDE,)),
            dma,
            dma((SIDE,)),
        ],
        compiler_params=pltpu.CompilerParams(
            collective_id=0, has_side_effects=True, vmem_limit_bytes=50 << 20
        ),
    )(pair_map, k1a, wide(b1a), k1b, wide(b1b), k2a, wide(b2a), k2b, wide(b2b))


def solution(mesh):
    placed = (P(None, "row", "col"), P(), P(), P(), P(), P(), P(), P(), P())
    return jax.shard_map(
        shards, mesh=mesh, in_specs=placed, out_specs=P(None, "row", "col"), check_vma=False
    )
```

```python
import functools

import jax
import jax.numpy as jnp
from jax import lax
from jax.experimental import pallas as pl
from jax.experimental.pallas import tpu as pltpu
from jax.sharding import PartitionSpec as P

MESH = pl.DeviceIdType.MESH
F32, BF16 = jnp.float32, jnp.bfloat16
NT = (((1,), (1,)), ((), ()))
ROWS, COLS, CHAN, SIDE, QUAD = 32, 128, 64, 8, 4
ROW_PAD, COL_PAD, HID_ROW, HID_COL = 8, 16, 4, 8
NEIGHBOURS = [(dr, dc) for dr in (-1, 0, 1) for dc in (-1, 0, 1) if dr or dc]


def elu(v):
    return jnp.where(v > 0, v, jnp.exp(jnp.minimum(v, 0.0)) - 1.0)


def rounded(v):
    return v.astype(BF16).astype(F32)


def low_lanes(shape):
    return lax.broadcasted_iota(jnp.int32, shape, len(shape) - 1) < CHAN


def doubled(packed):
    turned = pltpu.roll(packed, CHAN, packed.ndim - 1)
    low = low_lanes(packed.shape)
    return jnp.where(low, packed, turned), jnp.where(low, turned, packed)


def paired(first, second):
    return jnp.where(low_lanes(first.shape), first, second)


def nearby(at, step):
    upper = step // 4
    middle = lax.rem(upper + step // 2, 2)
    return (
        lax.rem(at // 4 + upper, 2) * 4
        + lax.rem(at // 2 + middle, 2) * 2
        + lax.rem(at + step, 2)
    )


class Halo:
    def __init__(self, rows, frame, send, recv, send_sem, recv_sem, row, col):
        self.rows, self.frame = rows, frame
        self.send, self.recv = send, recv
        self.send_sem, self.recv_sem = send_sem, recv_sem
        self.row, self.col = row, col

    def parts(self, at):
        dr, dc = NEIGHBOURS[at]
        if dc == 0:
            return 0 if dr < 0 else 1, self.rows * 4
        if dr == 0:
            return 2 if dc < 0 else 3, 8
        return 4 + (dr > 0) * 2 + (dc > 0), self.rows // 4

    def copy(self, at):
        dr, dc = NEIGHBOURS[at]
        there = len(NEIGHBOURS) - 1 - at
        mine, count = self.parts(at)
        other, _ = self.parts(there)
        device = (lax.rem(self.row + dr + 32, 32), lax.rem(self.col + dc + SIDE, SIDE))
        return pltpu.make_async_remote_copy(
            self.send.at[mine, pl.ds(0, count)],
            self.recv.at[other, pl.ds(0, count)],
            self.send_sem.at[mine],
            self.recv_sem.at[other],
            device_id=device,
            device_id_type=MESH,
        )

    def incoming(self, at):
        mine, count = self.parts(at)
        there = self.recv.at[mine, pl.ds(0, count)]
        return pltpu.make_async_copy(there, there, self.recv_sem.at[mine])

    def pack(self):
        frame, rows = self.frame, self.rows
        for at, (dr, dc) in enumerate(NEIGHBOURS):
            mine, _ = self.parts(at)
            top = ROW_PAD if dr < 0 else ROW_PAD + ROWS - rows
            left = COL_PAD if dc < 0 else COL_PAD + COLS - 8
            if dc == 0:

                lines = frame[top : top + rows, COL_PAD : COL_PAD + COLS, :]
                both = paired(lines[:, :64], lines[:, 64:]).astype(BF16)
                self.send[mine, 0 : rows * 4] = both.reshape(rows * 4, 16, 128)
            else:
                base, many = (ROW_PAD, ROWS // 4) if dr == 0 else (top, rows // 4)

                for t in range(many):
                    block = frame[base + 4 * t : base + 4 * t + 4, left : left + 8, :]
                    both = paired(block[:2].reshape(16, 128), block[2:].reshape(16, 128))
                    self.send[mine, t] = both.astype(BF16)

    def start(self):
        for at in range(len(NEIGHBOURS)):
            self.copy(at).start()

    def finish(self):
        frame, rows = self.frame, self.rows
        for at, (dr, dc) in enumerate(NEIGHBOURS):
            self.incoming(at).wait()
            mine, _ = self.parts(at)
            inside = jnp.logical_and(
                jnp.logical_and(self.row + dr >= 0, self.row + dr < 32),
                jnp.logical_and(self.col + dc >= 0, self.col + dc < SIDE),
            )
            top = ROW_PAD - rows if dr < 0 else ROW_PAD + ROWS
            left = COL_PAD - 8 if dc < 0 else COL_PAD + COLS
            if dc == 0:

                for i in range(rows):
                    line = self.recv[mine, i * 4 : i * 4 + 4].reshape(64, 128).astype(F32)
                    first, second = doubled(jnp.where(inside, line, 0.0))
                    frame[top + i, COL_PAD : COL_PAD + 64, :] = first
                    frame[top + i, COL_PAD + 64 : COL_PAD + 128, :] = second
            else:
                base, many = (ROW_PAD, ROWS // 4) if dr == 0 else (top, rows // 4)

                for t in range(many):
                    block = self.recv[mine, t].astype(F32)
                    first, second = doubled(jnp.where(inside, block, 0.0))
                    i = base + 4 * t
                    frame[i : i + 2, left : left + 8, :] = first.reshape(2, 8, 128)
                    frame[i + 2 : i + 4, left : left + 8, :] = second.reshape(2, 8, 128)
        for at in range(len(NEIGHBOURS)):
            self.copy(at).wait_send()


def three_taps(kernel, ky, swapped=False):
    pick = lambda kx: kernel[kx, ky] if swapped else kernel[ky, kx]
    zeros = jnp.zeros((CHAN, CHAN), BF16)
    return jnp.concatenate([pick(0), pick(1), pick(2), zeros], axis=1)


def body(
    x_hbm, k1a_hbm, b1a_hbm, k1b_hbm, b1b_hbm, k2a_hbm, b2a_hbm, k2b_hbm, b2b_hbm, out_ref,
    x_ref, k1a, k1b, k2a, k2b, b1a, b1b, b2a, b2b, load_sem, flat, frame, slab, hidden, wide, block_y, outbox, transit, inbox,
    halo_send, halo_recv, w1a, w1b, w2a, w2b,
    halo_ss, halo_rs, ss1, rs1, ss2, rs2,
):
    row, col = lax.axis_index("row"), lax.axis_index("col")
    z, quarter = row // QUAD, lax.rem(row, QUAD)

    barrier = pltpu.get_barrier_semaphore()

    def greet(device):
        pl.semaphore_signal(barrier, inc=1, device_id=device, device_id_type=MESH)

    for dr, dc in NEIGHBOURS:
        greet((lax.rem(row + dr + 32, 32), lax.rem(col + dc + SIDE, SIDE)))

    def greet_plane(t, _):
        other = lax.rem(col + t, SIDE)
        for k in range(QUAD):

            @pl.when(jnp.logical_or(t > 0, quarter != k))
            def _():
                greet((z * QUAD + k, other))

        @pl.when(jnp.logical_or(col != z, t > 0))
        def _():
            greet((col * QUAD + quarter, other))

        return 0

    lax.fori_loop(0, SIDE, greet_plane, 0)
    waits = 8 + 31 + SIDE - jnp.where(col == z, 1, 0)

    loads = {}
    for at, (name, source, target) in enumerate(
        (
            ("x", x_hbm, x_ref), ("1a", k1a_hbm, k1a), ("b1a", b1a_hbm, b1a),
            ("1b", k1b_hbm, k1b), ("b1b", b1b_hbm, b1b), ("2a", k2a_hbm, k2a),
            ("b2a", b2a_hbm, b2a), ("2b", k2b_hbm, k2b), ("b2b", b2b_hbm, b2b),
        )
    ):
        loads[name] = pltpu.make_async_copy(source, target, load_sem.at[at])
        loads[name].start()

    loads["x"].wait()

    def widen(g, _):
        flat[pl.ds(g * 512, 512), :] = x_ref[pl.ds(g * 16, 16)].astype(F32).reshape(512, 128)
        return 0

    lax.fori_loop(0, CHAN // 16, widen, 0)
    same = lax.broadcasted_iota(jnp.int32, (COLS, COLS), 0) == lax.broadcasted_iota(
        jnp.int32, (COLS, COLS), 1
    )
    unit = same.astype(F32).astype(BF16)

    def turn(t, _):
        for u in range(8):
            i = t * 8 + u
            line = flat[pl.ds(i, CHAN, stride=ROWS), :].astype(BF16)
            both = jnp.concatenate([line, line], axis=0)
            frame[ROW_PAD + i, COL_PAD : COL_PAD + COLS, :] = lax.dot_general(
                unit, both, NT, preferred_element_type=F32
            )
        return 0

    lax.fori_loop(0, ROWS // 8, turn, 0)

    def prepare_one():
        for name in ("1a", "b1a", "1b", "b1b"):
            loads[name].wait()
        for ky in range(3):
            for target, kernel in ((w1a, k1a), (w1b, k1b)):
                taps = three_taps(kernel, ky)
                target[:, ky * 256 : ky * 256 + 256] = jnp.concatenate([taps, taps], axis=0)

    def prepare_two():
        for name in ("2a", "b2a", "2b", "b2b"):
            loads[name].wait()
        zeros = jnp.zeros((CHAN, CHAN), BF16)
        for ky in range(3):
            w2a[:, ky * 256 : ky * 256 + 256] = jnp.concatenate(
                [three_taps(k2a, ky), three_taps(k2a, ky, True)], axis=0
            )
            for kx in range(3):
                upper = jnp.concatenate([k2b[ky, kx], zeros], axis=1)
                lower = jnp.concatenate([zeros, k2b[kx, ky]], axis=1)
                at = ky * 384 + kx * 128
                w2b[:, at : at + 128] = jnp.concatenate([upper, lower], axis=0)

    def bias(ref):
        return jnp.concatenate([ref[...], ref[...]], axis=1)

    def clear_outside():
        @pl.when(row == 0)
        def _():
            hidden[0:HID_ROW] = jnp.zeros((HID_ROW, 144, 128), F32)

        @pl.when(row == 31)
        def _():
            hidden[HID_ROW + ROWS :] = jnp.zeros((HID_ROW, 144, 128), F32)

        @pl.when(col == 0)
        def _():
            hidden[:, 0:HID_COL, :] = jnp.zeros((ROWS + 2 * HID_ROW, HID_COL, 128), F32)

        @pl.when(col == SIDE - 1)
        def _():
            hidden[:, HID_COL + COLS :, :] = jnp.zeros((ROWS + 2 * HID_ROW, HID_COL, 128), F32)

    halo = Halo(4, frame, halo_send.at[0], halo_recv.at[0], halo_ss.at[0], halo_rs.at[0], row, col)
    halo.pack()
    pl.semaphore_wait(barrier, waits)
    halo.start()
    prepare_one()
    halo.finish()

    def shifted(d, top):
        def one(i, _):
            at = COL_PAD - HID_COL
            left = frame[top + i, at - d : at - d + 144, :]
            here = frame[top + i, at : at + 144, :]
            right = frame[top + i, at + d : at + d + 144, :]
            slab[top + i, :, 0:128] = paired(left, here).astype(BF16)
            slab[top + i, :, 128:256] = right.astype(BF16)
            return 0

        return one

    def conv_a(d, weights, bias_ref, step):
        def one(t, _):
            i = t * step - d
            lhs = jnp.concatenate(
                [
                    slab[pl.ds(i + ROW_PAD + (ky - 1) * d, step)].reshape(step * 144, 256)
                    for ky in range(3)
                ],
                axis=1,
            )
            total = lax.dot_general(lhs, weights[...], NT, preferred_element_type=F32)
            value = rounded(elu(total + bias(bias_ref)))
            hidden[pl.ds(i + HID_ROW, step)] = value.reshape(step, 144, 128)
            return 0

        return one

    lax.fori_loop(0, 40, shifted(2, ROW_PAD - 4), 0)
    lax.fori_loop(0, 9, conv_a(2, w1a, b1a, 4), 0)
    clear_outside()

    def hidden_taps(i, _):
        at = i + HID_ROW - 2
        left = hidden[at, HID_COL - 2 : HID_COL + 126, :]
        here = hidden[at, HID_COL : HID_COL + 128, :]
        right = hidden[at, HID_COL + 2 : HID_COL + 130, :]
        slab[i, 0:128, 0:128] = paired(left, here).astype(BF16)
        slab[i, 0:128, 128:256] = right.astype(BF16)
        return 0

    lax.fori_loop(0, 36, hidden_taps, 0)

    def conv_b_one(t, _):
        i = t * 4
        lhs = jnp.concatenate(
            [slab[pl.ds(i + 2 * ky, 4), 0:128, :].reshape(512, 256) for ky in range(3)], axis=1
        )
        total = lax.dot_general(lhs, w1b[...], NT, preferred_element_type=F32)
        here = frame[pl.ds(ROW_PAD + i, 4), COL_PAD : COL_PAD + COLS, :].reshape(512, 128)
        block_y[pl.ds(i * COLS, 512), :] = rounded(elu(here + total + bias(b1b)))
        return 0

    lax.fori_loop(0, ROWS // 4, conv_b_one, 0)

    def spread(t, _):
        via = nearby(col, t)
        for k in range(QUAD):
            for u in range(4):
                column = block_y[pl.ds(32 * k + 4 * via + u, ROWS, stride=COLS), :]
                outbox[via, k, u] = paired(column[:16], column[16:]).astype(BF16)
            alone = jnp.logical_and(t == 0, quarter == k)

            @pl.when(alone)
            def _():
                pltpu.make_async_copy(
                    outbox.at[via, k], transit.at[col, quarter], rs1.at[col]
                ).start()

            @pl.when(jnp.logical_not(alone))
            def _():
                pltpu.make_async_remote_copy(
                    outbox.at[via, k],
                    transit.at[col, quarter],
                    ss1,
                    rs1.at[col],
                    device_id=(z * QUAD + k, via),
                    device_id_type=MESH,
                ).start()

        return 0

    lax.fori_loop(0, SIDE, spread, 0)

    def forward(t, _):
        origin = nearby(col, t)
        pltpu.make_async_copy(transit.at[origin], transit.at[origin], rs1.at[origin]).wait()
        alone = jnp.logical_and(origin == z, col == z)

        @pl.when(alone)
        def _():
            pltpu.make_async_copy(transit.at[origin], inbox.at[col], rs2.at[col]).start()

        @pl.when(jnp.logical_not(alone))
        def _():
            pltpu.make_async_remote_copy(
                transit.at[origin],
                inbox.at[col],
                ss2,
                rs2.at[col],
                device_id=(origin * QUAD + quarter, z),
                device_id_type=MESH,
            ).start()

        return 0

    lax.fori_loop(0, SIDE, forward, 0)
    prepare_two()

    def arrive(t, _):
        via = nearby(z, t)
        pltpu.make_async_copy(inbox.at[via], inbox.at[via], rs2.at[via]).wait()
        for u in range(4):
            i = via * 4 + u
            for k in range(QUAD):
                mirror = doubled(inbox[via, k, u].astype(F32))
                for half in range(2):
                    j = 32 * k + 16 * half
                    own = block_y[pl.ds(pl.multiple_of(i * COLS + j, 16), 16), :]
                    frame[ROW_PAD + i, COL_PAD + j : COL_PAD + j + 16, :] = rounded(
                        (own + mirror[half]) * 0.5
                    )
        return 0

    lax.fori_loop(0, SIDE, arrive, 0)

    halo = Halo(8, frame, halo_send.at[1], halo_recv.at[1], halo_ss.at[1], halo_rs.at[1], row, col)
    halo.pack()
    halo.start()
    halo.finish()

    lax.fori_loop(0, 48, shifted(4, 0), 0)
    lax.fori_loop(0, 10, conv_a(4, w2a, b2a, 4), 0)
    clear_outside()

    def wide_taps(i, _):
        for kx in range(3):
            at = HID_COL + 4 * (kx - 1)
            wide[i, :, kx * 128 : kx * 128 + 128] = hidden[i, at : at + 128, :].astype(BF16)
        return 0

    lax.fori_loop(0, 40, wide_taps, 0)

    lane = lax.broadcasted_iota(jnp.int32, (CHAN, 128), 1)
    chan = lax.broadcasted_iota(jnp.int32, (CHAN, 128), 0)
    mean = jnp.where(jnp.logical_or(lane == chan, lane == chan + CHAN), 0.5, 0.0).astype(BF16)

    def conv_b_two(t, _):
        i = t * 4
        lhs = jnp.concatenate(
            [wide[pl.ds(i + 4 * ky, 4)].reshape(512, 384) for ky in range(3)], axis=1
        )
        total = lax.dot_general(lhs, w2b[...], NT, preferred_element_type=F32)
        here = frame[pl.ds(ROW_PAD + i, 4), COL_PAD : COL_PAD + COLS, :].reshape(512, 128)
        both = elu(here + total + bias(b2b)).astype(BF16)
        for u in range(4):
            line = both[u * COLS : (u + 1) * COLS]
            flat[pl.ds(i + u, CHAN, stride=ROWS), :] = lax.dot_general(
                mean, line, NT, preferred_element_type=F32
            )
        return 0

    lax.fori_loop(0, ROWS // 4, conv_b_two, 0)

    def narrow(g, _):
        out_ref[pl.ds(g * 8, 8)] = flat[pl.ds(g * 256, 256), :].reshape(8, ROWS, COLS).astype(BF16)
        return 0

    lax.fori_loop(0, CHAN // 8, narrow, 0)

    def sent_one(t, _):
        for k in range(QUAD):

            @pl.when(jnp.logical_not(jnp.logical_and(t == 0, quarter == k)))
            def _():
                pltpu.make_async_copy(outbox.at[0, 0], outbox.at[0, 0], ss1).wait()

        @pl.when(jnp.logical_or(t > 0, col != z))
        def _():
            pltpu.make_async_copy(transit.at[0], transit.at[0], ss2).wait()

        return 0

    lax.fori_loop(0, SIDE, sent_one, 0)


def shards(pair_map, k1a, b1a, k1b, b1b, k2a, b2a, k2b, b2b):
    wide = lambda b: b.reshape(1, CHAN)
    vmem = pl.BlockSpec(memory_space=pltpu.VMEM)
    dma, regular = pltpu.SemaphoreType.DMA, pltpu.SemaphoreType.REGULAR
    return pl.pallas_call(
        body,
        out_shape=jax.ShapeDtypeStruct((CHAN, ROWS, COLS), BF16),
        in_specs=[pl.BlockSpec(memory_space=pl.ANY)] * 9,
        out_specs=vmem,
        scratch_shapes=[
            pltpu.VMEM((CHAN, ROWS, COLS), BF16),
            *[pltpu.VMEM((3, 3, CHAN, CHAN), BF16) for _ in range(4)],
            *[pltpu.VMEM((1, CHAN), F32) for _ in range(4)],
            dma((9,)),
            pltpu.VMEM((CHAN * ROWS, COLS), F32),
            pltpu.VMEM((ROWS + 2 * ROW_PAD, COLS + 2 * COL_PAD, 128), F32),
            pltpu.VMEM((ROWS + 2 * ROW_PAD, 144, 256), BF16),
            pltpu.VMEM((ROWS + 2 * HID_ROW, 144, 128), F32),
            pltpu.VMEM((ROWS + 2 * HID_ROW, COLS, 384), BF16),
            pltpu.VMEM((ROWS * COLS, 128), F32),
            pltpu.VMEM((SIDE, QUAD, 4, 16, 128), BF16),
            pltpu.VMEM((SIDE, QUAD, 4, 16, 128), BF16),
            pltpu.VMEM((SIDE, QUAD, 4, 16, 128), BF16),
            pltpu.VMEM((2, 8, 32, 16, 128), BF16),
            pltpu.VMEM((2, 8, 32, 16, 128), BF16),
            pltpu.VMEM((128, 768), BF16),
            pltpu.VMEM((128, 768), BF16),
            pltpu.VMEM((128, 768), BF16),
            pltpu.VMEM((128, 1152), BF16),
            dma((2, 8)),
            dma((2, 8)),
            dma,
            dma((SIDE,)),
            dma,
            dma((SIDE,)),
        ],
        compiler_params=pltpu.CompilerParams(
            collective_id=0, has_side_effects=True, vmem_limit_bytes=50 << 20
        ),
    )(pair_map, k1a, wide(b1a), k1b, wide(b1b), k2a, wide(b2a), k2b, wide(b2b))


def solution(mesh):
    placed = (P(None, "row", "col"), P(), P(), P(), P(), P(), P(), P(), P())
    return jax.shard_map(
        shards, mesh=mesh, in_specs=placed, out_specs=P(None, "row", "col"), check_vma=False
    )
```

```python
import functools

import jax
import jax.numpy as jnp
from jax import lax
from jax.experimental import pallas as pl
from jax.experimental.pallas import tpu as pltpu
from jax.sharding import PartitionSpec as P

MESH = pl.DeviceIdType.MESH
F32, BF16 = jnp.float32, jnp.bfloat16
NT = (((1,), (1,)), ((), ()))
ROWS, COLS, CHAN, SIDE, QUAD = 32, 128, 64, 8, 4
ROW_PAD, COL_PAD, HID_ROW, HID_COL = 8, 16, 4, 8
NEIGHBOURS = [(-1, 0), (-1, -1), (-1, 1), (0, -1), (0, 1), (1, -1), (1, 1), (1, 0)]
ORDER = [0, 7, 1, 2, 5, 6, 3, 4]
SIDEWAYS, OTHERS = [3, 4], [0, 7, 1, 2, 5, 6]


def elu(v):
    return jnp.where(v > 0, v, jnp.exp(jnp.minimum(v, 0.0)) - 1.0)


def rounded(v):
    return v.astype(BF16).astype(F32)


def low_lanes(shape):
    return lax.broadcasted_iota(jnp.int32, shape, len(shape) - 1) < CHAN


def doubled(packed):
    turned = pltpu.roll(packed, CHAN, packed.ndim - 1)
    low = low_lanes(packed.shape)
    return jnp.where(low, packed, turned), jnp.where(low, turned, packed)


def paired(first, second):
    return jnp.where(low_lanes(first.shape), first, second)


def nearby(at, step):
    upper = step // 4
    middle = lax.rem(upper + step // 2, 2)
    return (
        lax.rem(at // 4 + upper, 2) * 4
        + lax.rem(at // 2 + middle, 2) * 2
        + lax.rem(at + step, 2)
    )


class Halo:
    def __init__(self, rows, frame, send, recv, send_sem, recv_sem, row, col):
        self.rows, self.frame = rows, frame
        self.send, self.recv = send, recv
        self.send_sem, self.recv_sem = send_sem, recv_sem
        self.row, self.col = row, col

    def parts(self, at):
        dr, dc = NEIGHBOURS[at]
        if dc == 0:
            return 0 if dr < 0 else 1, self.rows * 4
        if dr == 0:
            return 2 if dc < 0 else 3, 8
        return 4 + (dr > 0) * 2 + (dc > 0), self.rows // 4

    def copy(self, at):
        dr, dc = NEIGHBOURS[at]
        there = len(NEIGHBOURS) - 1 - at
        mine, count = self.parts(at)
        other, _ = self.parts(there)
        device = (lax.rem(self.row + dr + 32, 32), lax.rem(self.col + dc + SIDE, SIDE))
        return pltpu.make_async_remote_copy(
            self.send.at[mine, pl.ds(0, count)],
            self.recv.at[other, pl.ds(0, count)],
            self.send_sem.at[mine],
            self.recv_sem.at[other],
            device_id=device,
            device_id_type=MESH,
        )

    def incoming(self, at):
        mine, count = self.parts(at)
        there = self.recv.at[mine, pl.ds(0, count)]
        return pltpu.make_async_copy(there, there, self.recv_sem.at[mine])

    def pack(self, start=False):
        frame, rows = self.frame, self.rows
        for at in ORDER:
            dr, dc = NEIGHBOURS[at]
            mine, _ = self.parts(at)
            top = ROW_PAD if dr < 0 else ROW_PAD + ROWS - rows
            left = COL_PAD if dc < 0 else COL_PAD + COLS - 8
            if dc == 0:

                lines = frame[top : top + rows, COL_PAD : COL_PAD + COLS, :]
                both = paired(lines[:, :64], lines[:, 64:]).astype(BF16)
                self.send[mine, 0 : rows * 4] = both.reshape(rows * 4, 16, 128)
            else:
                base, many = (ROW_PAD, ROWS // 4) if dr == 0 else (top, rows // 4)

                for t in range(many):
                    block = frame[base + 4 * t : base + 4 * t + 4, left : left + 8, :]
                    both = paired(block[:2].reshape(16, 128), block[2:].reshape(16, 128))
                    self.send[mine, t] = both.astype(BF16)
            if start:
                self.copy(at).start()

    def start(self):
        for at in ORDER:
            self.copy(at).start()

    def finish(self, which):
        frame, rows = self.frame, self.rows
        for at in which:
            dr, dc = NEIGHBOURS[at]
            self.incoming(at).wait()
            mine, _ = self.parts(at)
            inside = jnp.logical_and(
                jnp.logical_and(self.row + dr >= 0, self.row + dr < 32),
                jnp.logical_and(self.col + dc >= 0, self.col + dc < SIDE),
            )
            top = ROW_PAD - rows if dr < 0 else ROW_PAD + ROWS
            left = COL_PAD - 8 if dc < 0 else COL_PAD + COLS
            if dc == 0:

                for i in range(rows):
                    line = self.recv[mine, i * 4 : i * 4 + 4].reshape(64, 128).astype(F32)
                    first, second = doubled(jnp.where(inside, line, 0.0))
                    frame[top + i, COL_PAD : COL_PAD + 64, :] = first
                    frame[top + i, COL_PAD + 64 : COL_PAD + 128, :] = second
            else:
                base, many = (ROW_PAD, ROWS // 4) if dr == 0 else (top, rows // 4)

                for t in range(many):
                    block = self.recv[mine, t].astype(F32)
                    first, second = doubled(jnp.where(inside, block, 0.0))
                    i = base + 4 * t
                    frame[i : i + 2, left : left + 8, :] = first.reshape(2, 8, 128)
                    frame[i + 2 : i + 4, left : left + 8, :] = second.reshape(2, 8, 128)
        for at in which:
            self.copy(at).wait_send()


def three_taps(kernel, ky, swapped=False):
    pick = lambda kx: kernel[kx, ky] if swapped else kernel[ky, kx]
    zeros = jnp.zeros((CHAN, CHAN), BF16)
    return jnp.concatenate([pick(0), pick(1), pick(2), zeros], axis=1)


def body(
    x_hbm, k1a_hbm, b1a_hbm, k1b_hbm, b1b_hbm, k2a_hbm, b2a_hbm, k2b_hbm, b2b_hbm, out_ref,
    x_ref, k1a, k1b, k2a, k2b, b1a, b1b, b2a, b2b, load_sem, flat, frame, slab, hidden, wide, block_y, outbox, transit, inbox,
    halo_send, halo_recv, w1a, w1b, w2a, w2b,
    halo_ss, halo_rs, ss1, rs1, ss2, rs2,
):
    row, col = lax.axis_index("row"), lax.axis_index("col")
    z, quarter = row // QUAD, lax.rem(row, QUAD)

    barrier = pltpu.get_barrier_semaphore()

    def greet(device):
        pl.semaphore_signal(barrier, inc=1, device_id=device, device_id_type=MESH)

    for dr, dc in NEIGHBOURS:
        greet((lax.rem(row + dr + 32, 32), lax.rem(col + dc + SIDE, SIDE)))

    def greet_plane(t, _):
        other = lax.rem(col + t, SIDE)
        for k in range(QUAD):

            @pl.when(jnp.logical_or(t > 0, quarter != k))
            def _():
                greet((z * QUAD + k, other))

        @pl.when(jnp.logical_or(col != z, t > 0))
        def _():
            greet((col * QUAD + quarter, other))

        return 0

    lax.fori_loop(0, SIDE, greet_plane, 0)
    waits = 8 + 31 + SIDE - jnp.where(col == z, 1, 0)

    loads = {}
    for at, (name, source, target) in enumerate(
        (
            ("x", x_hbm, x_ref), ("1a", k1a_hbm, k1a), ("b1a", b1a_hbm, b1a),
            ("1b", k1b_hbm, k1b), ("b1b", b1b_hbm, b1b), ("2a", k2a_hbm, k2a),
            ("b2a", b2a_hbm, b2a), ("2b", k2b_hbm, k2b), ("b2b", b2b_hbm, b2b),
        )
    ):
        loads[name] = pltpu.make_async_copy(source, target, load_sem.at[at])
        loads[name].start()

    loads["x"].wait()

    def widen(g, _):
        flat[pl.ds(g * 512, 512), :] = x_ref[pl.ds(g * 16, 16)].astype(F32).reshape(512, 128)
        return 0

    lax.fori_loop(0, CHAN // 16, widen, 0)
    same = lax.broadcasted_iota(jnp.int32, (COLS, COLS), 0) == lax.broadcasted_iota(
        jnp.int32, (COLS, COLS), 1
    )
    unit = same.astype(F32).astype(BF16)

    def turn(t, _):
        for u in range(8):
            i = t * 8 + u
            line = flat[pl.ds(i, CHAN, stride=ROWS), :].astype(BF16)
            both = jnp.concatenate([line, line], axis=0)
            frame[ROW_PAD + i, COL_PAD : COL_PAD + COLS, :] = lax.dot_general(
                unit, both, NT, preferred_element_type=F32
            )
        return 0

    lax.fori_loop(0, ROWS // 8, turn, 0)

    def prepare_one():
        for name in ("1a", "b1a", "1b", "b1b"):
            loads[name].wait()
        for ky in range(3):
            for target, kernel in ((w1a, k1a), (w1b, k1b)):
                taps = three_taps(kernel, ky)
                target[:, ky * 256 : ky * 256 + 256] = jnp.concatenate([taps, taps], axis=0)

    def prepare_two():
        for name in ("2a", "b2a", "2b", "b2b"):
            loads[name].wait()
        zeros = jnp.zeros((CHAN, CHAN), BF16)
        for ky in range(3):
            w2a[:, ky * 256 : ky * 256 + 256] = jnp.concatenate(
                [three_taps(k2a, ky), three_taps(k2a, ky, True)], axis=0
            )
            for kx in range(3):
                upper = jnp.concatenate([k2b[ky, kx], zeros], axis=1)
                lower = jnp.concatenate([zeros, k2b[kx, ky]], axis=1)
                at = ky * 384 + kx * 128
                w2b[:, at : at + 128] = jnp.concatenate([upper, lower], axis=0)

    def bias(ref):
        return jnp.concatenate([ref[...], ref[...]], axis=1)

    def clear_outside():
        @pl.when(row == 0)
        def _():
            hidden[0:HID_ROW] = jnp.zeros((HID_ROW, 144, 128), F32)

        @pl.when(row == 31)
        def _():
            hidden[HID_ROW + ROWS :] = jnp.zeros((HID_ROW, 144, 128), F32)

        @pl.when(col == 0)
        def _():
            hidden[:, 0:HID_COL, :] = jnp.zeros((ROWS + 2 * HID_ROW, HID_COL, 128), F32)

        @pl.when(col == SIDE - 1)
        def _():
            hidden[:, HID_COL + COLS :, :] = jnp.zeros((ROWS + 2 * HID_ROW, HID_COL, 128), F32)

    halo = Halo(4, frame, halo_send.at[0], halo_recv.at[0], halo_ss.at[0], halo_rs.at[0], row, col)
    halo.pack()
    pl.semaphore_wait(barrier, waits)
    halo.start()
    prepare_one()
    halo.finish(SIDEWAYS)

    def shifted(d, top):
        def one(t, _):
            at = COL_PAD - HID_COL
            for u in range(4):
                i = top + t * 4 + u
                left = frame[i, at - d : at - d + 144, :]
                here = frame[i, at : at + 144, :]
                right = frame[i, at + d : at + d + 144, :]
                slab[i, :, 0:128] = paired(left, here).astype(BF16)
                slab[i, :, 128:256] = right.astype(BF16)
            return 0

        return one

    def conv_a(d, weights, bias_ref, first, step):
        def one(t, _):
            i = first + t * step
            lhs = jnp.concatenate(
                [
                    slab[pl.ds(i + ROW_PAD + (ky - 1) * d, step)].reshape(step * 144, 256)
                    for ky in range(3)
                ],
                axis=1,
            )
            total = lax.dot_general(lhs, weights[...], NT, preferred_element_type=F32)
            value = rounded(elu(total + bias(bias_ref)))
            hidden[pl.ds(i + HID_ROW, step)] = value.reshape(step, 144, 128)
            return 0

        return one

    lax.fori_loop(0, 8, shifted(2, ROW_PAD), 0)
    lax.fori_loop(0, 2, conv_a(2, w1a, b1a, 2, 14), 0)
    halo.finish(OTHERS)
    lax.fori_loop(0, 1, shifted(2, ROW_PAD - 4), 0)
    lax.fori_loop(0, 1, shifted(2, ROW_PAD + 32), 0)
    lax.fori_loop(0, 1, conv_a(2, w1a, b1a, -2, 4), 0)
    lax.fori_loop(0, 1, conv_a(2, w1a, b1a, 30, 4), 0)
    clear_outside()

    def hidden_taps(t, _):
        for u in range(4):
            i = t * 4 + u
            at = i + HID_ROW - 2
            left = hidden[at, HID_COL - 2 : HID_COL + 126, :]
            here = hidden[at, HID_COL : HID_COL + 128, :]
            right = hidden[at, HID_COL + 2 : HID_COL + 130, :]
            slab[i, 0:128, 0:128] = paired(left, here).astype(BF16)
            slab[i, 0:128, 128:256] = right.astype(BF16)
        return 0

    lax.fori_loop(0, 9, hidden_taps, 0)

    def conv_b_one(t, _):
        i = t * 16
        lhs = jnp.concatenate(
            [slab[pl.ds(i + 2 * ky, 16), 0:128, :].reshape(2048, 256) for ky in range(3)], axis=1
        )
        total = lax.dot_general(lhs, w1b[...], NT, preferred_element_type=F32)
        here = frame[pl.ds(ROW_PAD + i, 16), COL_PAD : COL_PAD + COLS, :].reshape(2048, 128)
        block_y[pl.ds(i * COLS, 2048), :] = rounded(elu(here + total + bias(b1b)))
        return 0

    lax.fori_loop(0, ROWS // 16, conv_b_one, 0)

    def spread(t, _):
        via = nearby(col, t)
        for k in range(QUAD):
            for u in range(4):
                column = block_y[pl.ds(32 * k + 4 * via + u, ROWS, stride=COLS), :]
                outbox[via, k, u] = paired(column[:16], column[16:]).astype(BF16)
            alone = jnp.logical_and(t == 0, quarter == k)

            @pl.when(alone)
            def _():
                pltpu.make_async_copy(
                    outbox.at[via, k], transit.at[col, quarter], rs1.at[col]
                ).start()

            @pl.when(jnp.logical_not(alone))
            def _():
                pltpu.make_async_remote_copy(
                    outbox.at[via, k],
                    transit.at[col, quarter],
                    ss1,
                    rs1.at[col],
                    device_id=(z * QUAD + k, via),
                    device_id_type=MESH,
                ).start()

        return 0

    lax.fori_loop(0, SIDE, spread, 0)

    def forward(t, _):
        origin = nearby(col, t)
        pltpu.make_async_copy(transit.at[origin], transit.at[origin], rs1.at[origin]).wait()
        alone = jnp.logical_and(origin == z, col == z)

        @pl.when(alone)
        def _():
            pltpu.make_async_copy(transit.at[origin], inbox.at[col], rs2.at[col]).start()

        @pl.when(jnp.logical_not(alone))
        def _():
            pltpu.make_async_remote_copy(
                transit.at[origin],
                inbox.at[col],
                ss2,
                rs2.at[col],
                device_id=(origin * QUAD + quarter, z),
                device_id_type=MESH,
            ).start()

        return 0

    lax.fori_loop(0, SIDE, forward, 0)
    prepare_two()

    def arrive(t, _):
        via = nearby(z, t)
        pltpu.make_async_copy(inbox.at[via], inbox.at[via], rs2.at[via]).wait()
        for u in range(4):
            i = via * 4 + u
            for k in range(QUAD):
                mirror = doubled(inbox[via, k, u].astype(F32))
                for half in range(2):
                    j = 32 * k + 16 * half
                    own = block_y[pl.ds(pl.multiple_of(i * COLS + j, 16), 16), :]
                    frame[ROW_PAD + i, COL_PAD + j : COL_PAD + j + 16, :] = rounded(
                        (own + mirror[half]) * 0.5
                    )
        return 0

    lax.fori_loop(0, SIDE, arrive, 0)

    halo = Halo(8, frame, halo_send.at[1], halo_recv.at[1], halo_ss.at[1], halo_rs.at[1], row, col)
    halo.pack(True)
    halo.finish(SIDEWAYS)

    lax.fori_loop(0, 8, shifted(4, ROW_PAD), 0)
    lax.fori_loop(0, 2, conv_a(4, w2a, b2a, 4, 12), 0)
    halo.finish(OTHERS)
    lax.fori_loop(0, 2, shifted(4, 0), 0)
    lax.fori_loop(0, 2, shifted(4, ROW_PAD + 32), 0)
    lax.fori_loop(0, 1, conv_a(4, w2a, b2a, -4, 8), 0)
    lax.fori_loop(0, 1, conv_a(4, w2a, b2a, 28, 8), 0)
    clear_outside()

    def wide_taps(t, _):
        for u in range(4):
            i = t * 4 + u
            for kx in range(3):
                at = HID_COL + 4 * (kx - 1)
                wide[i, :, kx * 128 : kx * 128 + 128] = hidden[i, at : at + 128, :].astype(BF16)
        return 0

    lax.fori_loop(0, 10, wide_taps, 0)

    lane = lax.broadcasted_iota(jnp.int32, (CHAN, 128), 1)
    chan = lax.broadcasted_iota(jnp.int32, (CHAN, 128), 0)
    mean = jnp.where(jnp.logical_or(lane == chan, lane == chan + CHAN), 0.5, 0.0).astype(BF16)

    def conv_b_two(t, _):
        i = t * 8
        lhs = jnp.concatenate(
            [wide[pl.ds(i + 4 * ky, 8)].reshape(1024, 384) for ky in range(3)], axis=1
        )
        total = lax.dot_general(lhs, w2b[...], NT, preferred_element_type=F32)
        here = frame[pl.ds(ROW_PAD + i, 8), COL_PAD : COL_PAD + COLS, :].reshape(1024, 128)
        both = elu(here + total + bias(b2b)).astype(BF16)
        for u in range(8):
            line = both[u * COLS : (u + 1) * COLS]
            flat[pl.ds(i + u, CHAN, stride=ROWS), :] = lax.dot_general(
                mean, line, NT, preferred_element_type=F32
            )
        return 0

    lax.fori_loop(0, ROWS // 8, conv_b_two, 0)

    def narrow(g, _):
        out_ref[pl.ds(g * 8, 8)] = flat[pl.ds(g * 256, 256), :].reshape(8, ROWS, COLS).astype(BF16)
        return 0

    lax.fori_loop(0, CHAN // 8, narrow, 0)

    def sent_one(t, _):
        for k in range(QUAD):

            @pl.when(jnp.logical_not(jnp.logical_and(t == 0, quarter == k)))
            def _():
                pltpu.make_async_copy(outbox.at[0, 0], outbox.at[0, 0], ss1).wait()

        @pl.when(jnp.logical_or(t > 0, col != z))
        def _():
            pltpu.make_async_copy(transit.at[0], transit.at[0], ss2).wait()

        return 0

    lax.fori_loop(0, SIDE, sent_one, 0)


def shards(pair_map, k1a, b1a, k1b, b1b, k2a, b2a, k2b, b2b):
    wide = lambda b: b.reshape(1, CHAN)
    vmem = pl.BlockSpec(memory_space=pltpu.VMEM)
    dma, regular = pltpu.SemaphoreType.DMA, pltpu.SemaphoreType.REGULAR
    return pl.pallas_call(
        body,
        out_shape=jax.ShapeDtypeStruct((CHAN, ROWS, COLS), BF16),
        in_specs=[pl.BlockSpec(memory_space=pl.ANY)] * 9,
        out_specs=vmem,
        scratch_shapes=[
            pltpu.VMEM((CHAN, ROWS, COLS), BF16),
            *[pltpu.VMEM((3, 3, CHAN, CHAN), BF16) for _ in range(4)],
            *[pltpu.VMEM((1, CHAN), F32) for _ in range(4)],
            dma((9,)),
            pltpu.VMEM((CHAN * ROWS, COLS), F32),
            pltpu.VMEM((ROWS + 2 * ROW_PAD, COLS + 2 * COL_PAD, 128), F32),
            pltpu.VMEM((ROWS + 2 * ROW_PAD, 144, 256), BF16),
            pltpu.VMEM((ROWS + 2 * HID_ROW, 144, 128), F32),
            pltpu.VMEM((ROWS + 2 * HID_ROW, COLS, 384), BF16),
            pltpu.VMEM((ROWS * COLS, 128), F32),
            pltpu.VMEM((SIDE, QUAD, 4, 16, 128), BF16),
            pltpu.VMEM((SIDE, QUAD, 4, 16, 128), BF16),
            pltpu.VMEM((SIDE, QUAD, 4, 16, 128), BF16),
            pltpu.VMEM((2, 8, 32, 16, 128), BF16),
            pltpu.VMEM((2, 8, 32, 16, 128), BF16),
            pltpu.VMEM((128, 768), BF16),
            pltpu.VMEM((128, 768), BF16),
            pltpu.VMEM((128, 768), BF16),
            pltpu.VMEM((128, 1152), BF16),
            dma((2, 8)),
            dma((2, 8)),
            dma,
            dma((SIDE,)),
            dma,
            dma((SIDE,)),
        ],
        compiler_params=pltpu.CompilerParams(
            collective_id=0, has_side_effects=True, vmem_limit_bytes=50 << 20
        ),
    )(pair_map, k1a, wide(b1a), k1b, wide(b1b), k2a, wide(b2a), k2b, wide(b2b))


def solution(mesh):
    placed = (P(None, "row", "col"), P(), P(), P(), P(), P(), P(), P(), P())
    return jax.shard_map(
        shards, mesh=mesh, in_specs=placed, out_specs=P(None, "row", "col"), check_vma=False
    )
```

```python
import functools

import jax
import jax.numpy as jnp
from jax import lax
from jax.experimental import pallas as pl
from jax.experimental.pallas import tpu as pltpu
from jax.sharding import PartitionSpec as P

MESH = pl.DeviceIdType.MESH
F32, BF16 = jnp.float32, jnp.bfloat16
NT = (((1,), (1,)), ((), ()))
ROWS, COLS, CHAN, SIDE, QUAD = 32, 128, 64, 8, 4
ROW_PAD, COL_PAD, HID_ROW, HID_COL = 8, 16, 4, 8
NEIGHBOURS = [(-1, 0), (-1, -1), (-1, 1), (0, -1), (0, 1), (1, -1), (1, 1), (1, 0)]
ORDER = [0, 7, 1, 2, 5, 6, 3, 4]
SIDEWAYS, OTHERS = [3, 4], [0, 7, 1, 2, 5, 6]


def elu(v):
    return jnp.where(v > 0, v, jnp.exp(jnp.minimum(v, 0.0)) - 1.0)


def rounded(v):
    return v.astype(BF16).astype(F32)


def low_lanes(shape):
    return lax.broadcasted_iota(jnp.int32, shape, len(shape) - 1) < CHAN


def doubled(packed):
    turned = pltpu.roll(packed, CHAN, packed.ndim - 1)
    low = low_lanes(packed.shape)
    return jnp.where(low, packed, turned), jnp.where(low, turned, packed)


def paired(first, second):
    return jnp.where(low_lanes(first.shape), first, second)


def nearby(at, step):
    upper = step // 4
    middle = lax.rem(upper + step // 2, 2)
    return (
        lax.rem(at // 4 + upper, 2) * 4
        + lax.rem(at // 2 + middle, 2) * 2
        + lax.rem(at + step, 2)
    )


def rows_at(step):
    return 2 * lax.rem(3 * (step // 2), 4) + lax.rem(step, 2)


class Halo:
    def __init__(self, rows, frame, send, recv, send_sem, recv_sem, row, col):
        self.rows, self.frame = rows, frame
        self.send, self.recv = send, recv
        self.send_sem, self.recv_sem = send_sem, recv_sem
        self.row, self.col = row, col

    def parts(self, at):
        dr, dc = NEIGHBOURS[at]
        if dc == 0:
            return 0 if dr < 0 else 1, self.rows * 4
        if dr == 0:
            return 2 if dc < 0 else 3, 8
        return 4 + (dr > 0) * 2 + (dc > 0), self.rows // 4

    def copy(self, at):
        dr, dc = NEIGHBOURS[at]
        there = len(NEIGHBOURS) - 1 - at
        mine, count = self.parts(at)
        other, _ = self.parts(there)
        device = (lax.rem(self.row + dr + 32, 32), lax.rem(self.col + dc + SIDE, SIDE))
        return pltpu.make_async_remote_copy(
            self.send.at[mine, pl.ds(0, count)],
            self.recv.at[other, pl.ds(0, count)],
            self.send_sem.at[mine],
            self.recv_sem.at[other],
            device_id=device,
            device_id_type=MESH,
        )

    def incoming(self, at):
        mine, count = self.parts(at)
        there = self.recv.at[mine, pl.ds(0, count)]
        return pltpu.make_async_copy(there, there, self.recv_sem.at[mine])

    def pack(self, which, start=False):
        frame, rows = self.frame, self.rows
        for at in which:
            dr, dc = NEIGHBOURS[at]
            mine, _ = self.parts(at)
            top = ROW_PAD if dr < 0 else ROW_PAD + ROWS - rows
            left = COL_PAD if dc < 0 else COL_PAD + COLS - 8
            if dc == 0:

                lines = frame[top : top + rows, COL_PAD : COL_PAD + COLS, :]
                both = paired(lines[:, :64], lines[:, 64:]).astype(BF16)
                self.send[mine, 0 : rows * 4] = both.reshape(rows * 4, 16, 128)
            else:
                base, many = (ROW_PAD, ROWS // 4) if dr == 0 else (top, rows // 4)

                for t in range(many):
                    block = frame[base + 4 * t : base + 4 * t + 4, left : left + 8, :]
                    both = paired(block[:2].reshape(16, 128), block[2:].reshape(16, 128))
                    self.send[mine, t] = both.astype(BF16)
            if start:
                self.copy(at).start()

    def start(self):
        for at in ORDER:
            self.copy(at).start()

    def finish(self, which):
        frame, rows = self.frame, self.rows
        for at in which:
            dr, dc = NEIGHBOURS[at]
            self.incoming(at).wait()
            mine, _ = self.parts(at)
            inside = jnp.logical_and(
                jnp.logical_and(self.row + dr >= 0, self.row + dr < 32),
                jnp.logical_and(self.col + dc >= 0, self.col + dc < SIDE),
            )
            top = ROW_PAD - rows if dr < 0 else ROW_PAD + ROWS
            left = COL_PAD - 8 if dc < 0 else COL_PAD + COLS
            if dc == 0:

                for i in range(rows):
                    line = self.recv[mine, i * 4 : i * 4 + 4].reshape(64, 128).astype(F32)
                    first, second = doubled(jnp.where(inside, line, 0.0))
                    frame[top + i, COL_PAD : COL_PAD + 64, :] = first
                    frame[top + i, COL_PAD + 64 : COL_PAD + 128, :] = second
            else:
                base, many = (ROW_PAD, ROWS // 4) if dr == 0 else (top, rows // 4)

                for t in range(many):
                    block = self.recv[mine, t].astype(F32)
                    first, second = doubled(jnp.where(inside, block, 0.0))
                    i = base + 4 * t
                    frame[i : i + 2, left : left + 8, :] = first.reshape(2, 8, 128)
                    frame[i + 2 : i + 4, left : left + 8, :] = second.reshape(2, 8, 128)
        for at in which:
            self.copy(at).wait_send()


def three_taps(kernel, ky, swapped=False):
    pick = lambda kx: kernel[kx, ky] if swapped else kernel[ky, kx]
    zeros = jnp.zeros((CHAN, CHAN), BF16)
    return jnp.concatenate([pick(0), pick(1), pick(2), zeros], axis=1)


def body(
    x_hbm, k1a_hbm, b1a_hbm, k1b_hbm, b1b_hbm, k2a_hbm, b2a_hbm, k2b_hbm, b2b_hbm, out_ref,
    x_ref, k1a, k1b, k2a, k2b, b1a, b1b, b2a, b2b, load_sem, flat, frame, slab, hidden, wide, block_y, outbox, transit, inbox,
    halo_send, halo_recv, w1a, w1b, w2a, w2b,
    halo_ss, halo_rs, ss1, rs1, ss2, rs2,
):
    row, col = lax.axis_index("row"), lax.axis_index("col")
    z, quarter = row // QUAD, lax.rem(row, QUAD)

    barrier = pltpu.get_barrier_semaphore()

    def greet(device):
        pl.semaphore_signal(barrier, inc=1, device_id=device, device_id_type=MESH)

    for dr, dc in NEIGHBOURS:
        greet((lax.rem(row + dr + 32, 32), lax.rem(col + dc + SIDE, SIDE)))

    def greet_plane(t, _):
        other = lax.rem(col + t, SIDE)
        for k in range(QUAD):

            @pl.when(jnp.logical_or(t > 0, quarter != k))
            def _():
                greet((z * QUAD + k, other))

        @pl.when(jnp.logical_or(col != z, t > 0))
        def _():
            greet((col * QUAD + quarter, other))

        return 0

    lax.fori_loop(0, SIDE, greet_plane, 0)
    waits = 8 + 31 + SIDE - jnp.where(col == z, 1, 0)

    loads = {}
    for at, (name, source, target) in enumerate(
        (
            ("x", x_hbm, x_ref), ("1a", k1a_hbm, k1a), ("b1a", b1a_hbm, b1a),
            ("1b", k1b_hbm, k1b), ("b1b", b1b_hbm, b1b), ("2a", k2a_hbm, k2a),
            ("b2a", b2a_hbm, b2a), ("2b", k2b_hbm, k2b), ("b2b", b2b_hbm, b2b),
        )
    ):
        loads[name] = pltpu.make_async_copy(source, target, load_sem.at[at])
        loads[name].start()

    loads["x"].wait()

    def widen(g, _):
        flat[pl.ds(g * 512, 512), :] = x_ref[pl.ds(g * 16, 16)].astype(F32).reshape(512, 128)
        return 0

    lax.fori_loop(0, CHAN // 16, widen, 0)
    same = lax.broadcasted_iota(jnp.int32, (COLS, COLS), 0) == lax.broadcasted_iota(
        jnp.int32, (COLS, COLS), 1
    )
    unit = same.astype(F32).astype(BF16)

    def turn(t, _):
        for u in range(8):
            i = t * 8 + u
            line = flat[pl.ds(i, CHAN, stride=ROWS), :].astype(BF16)
            both = jnp.concatenate([line, line], axis=0)
            frame[ROW_PAD + i, COL_PAD : COL_PAD + COLS, :] = lax.dot_general(
                unit, both, NT, preferred_element_type=F32
            )
        return 0

    lax.fori_loop(0, ROWS // 8, turn, 0)

    def prepare_one():
        for name in ("1a", "b1a", "1b", "b1b"):
            loads[name].wait()
        for ky in range(3):
            for target, kernel in ((w1a, k1a), (w1b, k1b)):
                taps = three_taps(kernel, ky)
                target[:, ky * 256 : ky * 256 + 256] = jnp.concatenate([taps, taps], axis=0)

    def prepare_two():
        for name in ("2a", "b2a", "2b", "b2b"):
            loads[name].wait()
        zeros = jnp.zeros((CHAN, CHAN), BF16)
        for ky in range(3):
            w2a[:, ky * 256 : ky * 256 + 256] = jnp.concatenate(
                [three_taps(k2a, ky), three_taps(k2a, ky, True)], axis=0
            )
            for kx in range(3):
                upper = jnp.concatenate([k2b[ky, kx], zeros], axis=1)
                lower = jnp.concatenate([zeros, k2b[kx, ky]], axis=1)
                at = ky * 384 + kx * 128
                w2b[:, at : at + 128] = jnp.concatenate([upper, lower], axis=0)

    def bias(ref):
        return jnp.concatenate([ref[...], ref[...]], axis=1)

    def clear_outside():
        @pl.when(row == 0)
        def _():
            hidden[0:HID_ROW] = jnp.zeros((HID_ROW, 144, 128), F32)

        @pl.when(row == 31)
        def _():
            hidden[HID_ROW + ROWS :] = jnp.zeros((HID_ROW, 144, 128), F32)

        @pl.when(col == 0)
        def _():
            hidden[:, 0:HID_COL, :] = jnp.zeros((ROWS + 2 * HID_ROW, HID_COL, 128), F32)

        @pl.when(col == SIDE - 1)
        def _():
            hidden[:, HID_COL + COLS :, :] = jnp.zeros((ROWS + 2 * HID_ROW, HID_COL, 128), F32)

    halo = Halo(4, frame, halo_send.at[0], halo_recv.at[0], halo_ss.at[0], halo_rs.at[0], row, col)
    halo.pack(ORDER)
    pl.semaphore_wait(barrier, waits)
    halo.start()
    prepare_one()

    everywhere, borders = ((0, 144),), ((0, 16), (128, 144))

    def shifted(d, top, spans=everywhere):
        def one(t, _):
            for u in range(4):
                i = top + t * 4 + u
                for low, high in spans:
                    at, many = COL_PAD - HID_COL + low, high - low
                    left = frame[i, at - d : at - d + many, :]
                    here = frame[i, at : at + many, :]
                    right = frame[i, at + d : at + d + many, :]
                    slab[i, low:high, 0:128] = paired(left, here).astype(BF16)
                    slab[i, low:high, 128:256] = right.astype(BF16)
            return 0

        return one

    def conv_a(d, weights, bias_ref, first, step, spans=everywhere):
        def one(t, _):
            i = first + t * step
            for low, high in spans:
                many = high - low
                lhs = jnp.concatenate(
                    [
                        slab[pl.ds(i + ROW_PAD + ky * d, step), low:high, :].reshape(
                            step * many, 256
                        )
                        for ky in (-1, 0, 1)
                    ],
                    axis=1,
                )
                total = lax.dot_general(lhs, weights[...], NT, preferred_element_type=F32)
                value = rounded(elu(total + bias(bias_ref)))
                hidden[pl.ds(i + HID_ROW, step), low:high, :] = value.reshape(step, many, 128)
            return 0

        return one

    lax.fori_loop(0, 8, shifted(2, ROW_PAD), 0)
    lax.fori_loop(0, 2, conv_a(2, w1a, b1a, 2, 14), 0)
    halo.finish(SIDEWAYS)
    lax.fori_loop(0, 8, shifted(2, ROW_PAD, borders), 0)
    lax.fori_loop(0, 1, conv_a(2, w1a, b1a, 2, 28, borders), 0)
    halo.finish(OTHERS)
    lax.fori_loop(0, 1, shifted(2, ROW_PAD - 4), 0)
    lax.fori_loop(0, 1, shifted(2, ROW_PAD + 32), 0)
    lax.fori_loop(0, 1, conv_a(2, w1a, b1a, -2, 4), 0)
    lax.fori_loop(0, 1, conv_a(2, w1a, b1a, 30, 4), 0)
    clear_outside()

    def hidden_taps(t, _):
        for u in range(4):
            i = t * 4 + u
            at = i + HID_ROW - 2
            left = hidden[at, HID_COL - 2 : HID_COL + 126, :]
            here = hidden[at, HID_COL : HID_COL + 128, :]
            right = hidden[at, HID_COL + 2 : HID_COL + 130, :]
            slab[i, 0:128, 0:128] = paired(left, here).astype(BF16)
            slab[i, 0:128, 128:256] = right.astype(BF16)
        return 0

    lax.fori_loop(0, 9, hidden_taps, 0)

    def conv_b_one(t, _):
        i = t * 16
        lhs = jnp.concatenate(
            [slab[pl.ds(i + 2 * ky, 16), 0:128, :].reshape(2048, 256) for ky in range(3)], axis=1
        )
        total = lax.dot_general(lhs, w1b[...], NT, preferred_element_type=F32)
        here = frame[pl.ds(ROW_PAD + i, 16), COL_PAD : COL_PAD + COLS, :].reshape(2048, 128)
        block_y[pl.ds(i * COLS, 2048), :] = rounded(elu(here + total + bias(b1b)))
        return 0

    lax.fori_loop(0, ROWS // 16, conv_b_one, 0)

    def spread(t, _):
        via = nearby(col, t)
        for k in range(QUAD):
            for u in range(4):
                column = block_y[pl.ds(32 * k + 4 * rows_at(t) + u, ROWS, stride=COLS), :]
                outbox[via, k, u] = paired(column[:16], column[16:]).astype(BF16)
            alone = jnp.logical_and(t == 0, quarter == k)

            @pl.when(alone)
            def _():
                pltpu.make_async_copy(
                    outbox.at[via, k], transit.at[col, quarter], rs1.at[col]
                ).start()

            @pl.when(jnp.logical_not(alone))
            def _():
                pltpu.make_async_remote_copy(
                    outbox.at[via, k],
                    transit.at[col, quarter],
                    ss1,
                    rs1.at[col],
                    device_id=(z * QUAD + k, via),
                    device_id_type=MESH,
                ).start()

        return 0

    lax.fori_loop(0, SIDE, spread, 0)

    def forward(t, _):
        origin = nearby(col, t)
        pltpu.make_async_copy(transit.at[origin], transit.at[origin], rs1.at[origin]).wait()
        alone = jnp.logical_and(origin == z, col == z)

        @pl.when(alone)
        def _():
            pltpu.make_async_copy(transit.at[origin], inbox.at[col], rs2.at[col]).start()

        @pl.when(jnp.logical_not(alone))
        def _():
            pltpu.make_async_remote_copy(
                transit.at[origin],
                inbox.at[col],
                ss2,
                rs2.at[col],
                device_id=(origin * QUAD + quarter, z),
                device_id_type=MESH,
            ).start()

        return 0

    lax.fori_loop(0, SIDE, forward, 0)
    prepare_two()

    def arrive(t, _):
        via = nearby(z, t)
        pltpu.make_async_copy(inbox.at[via], inbox.at[via], rs2.at[via]).wait()
        for u in range(4):
            i = rows_at(t) * 4 + u
            for k in range(QUAD):
                mirror = doubled(inbox[via, k, u].astype(F32))
                for half in range(2):
                    j = 32 * k + 16 * half
                    own = block_y[pl.ds(pl.multiple_of(i * COLS + j, 16), 16), :]
                    frame[ROW_PAD + i, COL_PAD + j : COL_PAD + j + 16, :] = rounded(
                        (own + mirror[half]) * 0.5
                    )
        return 0

    halo = Halo(8, frame, halo_send.at[1], halo_recv.at[1], halo_ss.at[1], halo_rs.at[1], row, col)
    lax.fori_loop(0, SIDE // 2, arrive, 0)
    halo.pack(OTHERS, True)
    lax.fori_loop(SIDE // 2, SIDE, arrive, 0)
    halo.pack(SIDEWAYS, True)
    halo.finish(OTHERS)

    lax.fori_loop(0, 12, shifted(4, 0), 0)
    lax.fori_loop(0, 2, conv_a(4, w2a, b2a, -4, 20), 0)
    halo.finish(SIDEWAYS)
    lax.fori_loop(0, 12, shifted(4, 0, borders), 0)
    lax.fori_loop(0, 1, conv_a(4, w2a, b2a, -4, 40, borders), 0)
    clear_outside()

    def wide_taps(t, _):
        for u in range(4):
            i = t * 4 + u
            for kx in range(3):
                at = HID_COL + 4 * (kx - 1)
                wide[i, :, kx * 128 : kx * 128 + 128] = hidden[i, at : at + 128, :].astype(BF16)
        return 0

    lax.fori_loop(0, 10, wide_taps, 0)

    lane = lax.broadcasted_iota(jnp.int32, (CHAN, 128), 1)
    chan = lax.broadcasted_iota(jnp.int32, (CHAN, 128), 0)
    mean = jnp.where(jnp.logical_or(lane == chan, lane == chan + CHAN), 0.5, 0.0).astype(BF16)

    def conv_b_two(t, _):
        i = t * 8
        lhs = jnp.concatenate(
            [wide[pl.ds(i + 4 * ky, 8)].reshape(1024, 384) for ky in range(3)], axis=1
        )
        total = lax.dot_general(lhs, w2b[...], NT, preferred_element_type=F32)
        here = frame[pl.ds(ROW_PAD + i, 8), COL_PAD : COL_PAD + COLS, :].reshape(1024, 128)
        both = elu(here + total + bias(b2b)).astype(BF16)
        for u in range(8):
            line = both[u * COLS : (u + 1) * COLS]
            flat[pl.ds(i + u, CHAN, stride=ROWS), :] = lax.dot_general(
                mean, line, NT, preferred_element_type=F32
            )
        return 0

    lax.fori_loop(0, ROWS // 8, conv_b_two, 0)

    def narrow(g, _):
        out_ref[pl.ds(g * 8, 8)] = flat[pl.ds(g * 256, 256), :].reshape(8, ROWS, COLS).astype(BF16)
        return 0

    lax.fori_loop(0, CHAN // 8, narrow, 0)

    def sent_one(t, _):
        for k in range(QUAD):

            @pl.when(jnp.logical_not(jnp.logical_and(t == 0, quarter == k)))
            def _():
                pltpu.make_async_copy(outbox.at[0, 0], outbox.at[0, 0], ss1).wait()

        @pl.when(jnp.logical_or(t > 0, col != z))
        def _():
            pltpu.make_async_copy(transit.at[0], transit.at[0], ss2).wait()

        return 0

    lax.fori_loop(0, SIDE, sent_one, 0)


def shards(pair_map, k1a, b1a, k1b, b1b, k2a, b2a, k2b, b2b):
    wide = lambda b: b.reshape(1, CHAN)
    vmem = pl.BlockSpec(memory_space=pltpu.VMEM)
    dma, regular = pltpu.SemaphoreType.DMA, pltpu.SemaphoreType.REGULAR
    return pl.pallas_call(
        body,
        out_shape=jax.ShapeDtypeStruct((CHAN, ROWS, COLS), BF16),
        in_specs=[pl.BlockSpec(memory_space=pl.ANY)] * 9,
        out_specs=vmem,
        scratch_shapes=[
            pltpu.VMEM((CHAN, ROWS, COLS), BF16),
            *[pltpu.VMEM((3, 3, CHAN, CHAN), BF16) for _ in range(4)],
            *[pltpu.VMEM((1, CHAN), F32) for _ in range(4)],
            dma((9,)),
            pltpu.VMEM((CHAN * ROWS, COLS), F32),
            pltpu.VMEM((ROWS + 2 * ROW_PAD, COLS + 2 * COL_PAD, 128), F32),
            pltpu.VMEM((ROWS + 2 * ROW_PAD, 144, 256), BF16),
            pltpu.VMEM((ROWS + 2 * HID_ROW, 144, 128), F32),
            pltpu.VMEM((ROWS + 2 * HID_ROW, COLS, 384), BF16),
            pltpu.VMEM((ROWS * COLS, 128), F32),
            pltpu.VMEM((SIDE, QUAD, 4, 16, 128), BF16),
            pltpu.VMEM((SIDE, QUAD, 4, 16, 128), BF16),
            pltpu.VMEM((SIDE, QUAD, 4, 16, 128), BF16),
            pltpu.VMEM((2, 8, 32, 16, 128), BF16),
            pltpu.VMEM((2, 8, 32, 16, 128), BF16),
            pltpu.VMEM((128, 768), BF16),
            pltpu.VMEM((128, 768), BF16),
            pltpu.VMEM((128, 768), BF16),
            pltpu.VMEM((128, 1152), BF16),
            dma((2, 8)),
            dma((2, 8)),
            dma,
            dma((SIDE,)),
            dma,
            dma((SIDE,)),
        ],
        compiler_params=pltpu.CompilerParams(
            collective_id=0, has_side_effects=True, vmem_limit_bytes=50 << 20
        ),
    )(pair_map, k1a, wide(b1a), k1b, wide(b1b), k2a, wide(b2a), k2b, wide(b2b))


def solution(mesh):
    placed = (P(None, "row", "col"), P(), P(), P(), P(), P(), P(), P(), P())
    return jax.shard_map(
        shards, mesh=mesh, in_specs=placed, out_specs=P(None, "row", "col"), check_vma=False
    )
```

```python
import functools

import jax
import jax.numpy as jnp
from jax import lax
from jax.experimental import pallas as pl
from jax.experimental.pallas import tpu as pltpu
from jax.sharding import PartitionSpec as P

MESH = pl.DeviceIdType.MESH
F32, BF16 = jnp.float32, jnp.bfloat16
NT = (((1,), (1,)), ((), ()))
ROWS, COLS, CHAN, SIDE, QUAD = 32, 128, 64, 8, 4
ROW_PAD, COL_PAD, HID_ROW, HID_COL = 8, 16, 4, 8
NEIGHBOURS = [(-1, 0), (-1, -1), (-1, 1), (0, -1), (0, 1), (1, -1), (1, 1), (1, 0)]
ORDER = [0, 7, 1, 2, 5, 6, 3, 4]
SIDEWAYS, OTHERS = [3, 4], [0, 7, 1, 2, 5, 6]


def elu(v):
    return jnp.where(v > 0, v, jnp.exp(jnp.minimum(v, 0.0)) - 1.0)


def rounded(v):
    return v.astype(BF16).astype(F32)


def low_lanes(shape):
    return lax.broadcasted_iota(jnp.int32, shape, len(shape) - 1) < CHAN


def doubled(packed):
    turned = pltpu.roll(packed, CHAN, packed.ndim - 1)
    low = low_lanes(packed.shape)
    return jnp.where(low, packed, turned), jnp.where(low, turned, packed)


def paired(first, second):
    return jnp.where(low_lanes(first.shape), first, second)


def nearby(at, step):
    upper = step // 4
    middle = lax.rem(upper + step // 2, 2)
    return (
        lax.rem(at // 4 + upper, 2) * 4
        + lax.rem(at // 2 + middle, 2) * 2
        + lax.rem(at + step, 2)
    )


def rows_at(step):
    return 2 * lax.rem(3 * (step // 2), 4) + lax.rem(step, 2)


class Halo:
    def __init__(self, rows, frame, send, recv, send_sem, recv_sem, row, col):
        self.rows, self.frame = rows, frame
        self.send, self.recv = send, recv
        self.send_sem, self.recv_sem = send_sem, recv_sem
        self.row, self.col = row, col

    def parts(self, at):
        dr, dc = NEIGHBOURS[at]
        if dc == 0:
            return 0 if dr < 0 else 1, self.rows * 4
        if dr == 0:
            return 2 if dc < 0 else 3, 8
        return 4 + (dr > 0) * 2 + (dc > 0), self.rows // 4

    def copy(self, at):
        dr, dc = NEIGHBOURS[at]
        there = len(NEIGHBOURS) - 1 - at
        mine, count = self.parts(at)
        other, _ = self.parts(there)
        device = (lax.rem(self.row + dr + 32, 32), lax.rem(self.col + dc + SIDE, SIDE))
        return pltpu.make_async_remote_copy(
            self.send.at[mine, pl.ds(0, count)],
            self.recv.at[other, pl.ds(0, count)],
            self.send_sem.at[mine],
            self.recv_sem.at[other],
            device_id=device,
            device_id_type=MESH,
        )

    def incoming(self, at):
        mine, count = self.parts(at)
        there = self.recv.at[mine, pl.ds(0, count)]
        return pltpu.make_async_copy(there, there, self.recv_sem.at[mine])

    def pack(self, which, start=False):
        frame, rows = self.frame, self.rows
        for at in which:
            dr, dc = NEIGHBOURS[at]
            mine, _ = self.parts(at)
            top = ROW_PAD if dr < 0 else ROW_PAD + ROWS - rows
            left = COL_PAD if dc < 0 else COL_PAD + COLS - 8
            if dc == 0:

                lines = frame[top : top + rows, COL_PAD : COL_PAD + COLS, :]
                both = paired(lines[:, :64], lines[:, 64:]).astype(BF16)
                self.send[mine, 0 : rows * 4] = both.reshape(rows * 4, 16, 128)
            else:
                base, many = (ROW_PAD, ROWS // 4) if dr == 0 else (top, rows // 4)

                for t in range(many):
                    block = frame[base + 4 * t : base + 4 * t + 4, left : left + 8, :]
                    both = paired(block[:2].reshape(16, 128), block[2:].reshape(16, 128))
                    self.send[mine, t] = both.astype(BF16)
            if start:
                self.copy(at).start()

    def start(self):
        for at in ORDER:
            self.copy(at).start()

    def finish(self, which):
        frame, rows = self.frame, self.rows
        for at in which:
            dr, dc = NEIGHBOURS[at]
            self.incoming(at).wait()
            mine, _ = self.parts(at)
            inside = jnp.logical_and(
                jnp.logical_and(self.row + dr >= 0, self.row + dr < 32),
                jnp.logical_and(self.col + dc >= 0, self.col + dc < SIDE),
            )
            top = ROW_PAD - rows if dr < 0 else ROW_PAD + ROWS
            left = COL_PAD - 8 if dc < 0 else COL_PAD + COLS
            if dc == 0:

                for i in range(rows):
                    line = self.recv[mine, i * 4 : i * 4 + 4].reshape(64, 128).astype(F32)
                    first, second = doubled(jnp.where(inside, line, 0.0))
                    frame[top + i, COL_PAD : COL_PAD + 64, :] = first
                    frame[top + i, COL_PAD + 64 : COL_PAD + 128, :] = second
            else:
                base, many = (ROW_PAD, ROWS // 4) if dr == 0 else (top, rows // 4)

                for t in range(many):
                    block = self.recv[mine, t].astype(F32)
                    first, second = doubled(jnp.where(inside, block, 0.0))
                    i = base + 4 * t
                    frame[i : i + 2, left : left + 8, :] = first.reshape(2, 8, 128)
                    frame[i + 2 : i + 4, left : left + 8, :] = second.reshape(2, 8, 128)
        for at in which:
            self.copy(at).wait_send()


def three_taps(kernel, ky, swapped=False):
    pick = lambda kx: kernel[kx, ky] if swapped else kernel[ky, kx]
    zeros = jnp.zeros((CHAN, CHAN), BF16)
    return jnp.concatenate([pick(0), pick(1), pick(2), zeros], axis=1)


def body(
    x_hbm, k1a_hbm, b1a_hbm, k1b_hbm, b1b_hbm, k2a_hbm, b2a_hbm, k2b_hbm, b2b_hbm, out_ref,
    x_ref, k1a, k1b, k2a, k2b, b1a, b1b, b2a, b2b, load_sem, flat, frame, slab, hidden, wide, block_y, outbox, transit, inbox,
    halo_send, halo_recv, w1a, w1b, w2a, w2b,
    halo_ss, halo_rs, ss1, rs1, ss2, rs2,
):
    row, col = lax.axis_index("row"), lax.axis_index("col")
    z, quarter = row // QUAD, lax.rem(row, QUAD)

    loads = {"x": pltpu.make_async_copy(x_hbm, x_ref, load_sem.at[0])}
    loads["x"].start()

    barrier = pltpu.get_barrier_semaphore()

    def greet(device):
        pl.semaphore_signal(barrier, inc=1, device_id=device, device_id_type=MESH)

    for dr, dc in NEIGHBOURS:
        greet((lax.rem(row + dr + 32, 32), lax.rem(col + dc + SIDE, SIDE)))

    def greet_plane(t, _):
        other = lax.rem(col + t, SIDE)
        for k in range(QUAD):

            @pl.when(jnp.logical_or(t > 0, quarter != k))
            def _():
                greet((z * QUAD + k, other))

        @pl.when(jnp.logical_or(col != z, t > 0))
        def _():
            greet((col * QUAD + quarter, other))

        return 0

    lax.fori_loop(0, SIDE, greet_plane, 0)
    waits = 8 + 31 + SIDE - jnp.where(col == z, 1, 0)

    for at, (name, source, target) in enumerate(
        (
            ("1a", k1a_hbm, k1a), ("b1a", b1a_hbm, b1a),
            ("1b", k1b_hbm, k1b), ("b1b", b1b_hbm, b1b), ("2a", k2a_hbm, k2a),
            ("b2a", b2a_hbm, b2a), ("2b", k2b_hbm, k2b), ("b2b", b2b_hbm, b2b),
        )
    ):
        loads[name] = pltpu.make_async_copy(source, target, load_sem.at[at + 1])
        loads[name].start()

    loads["x"].wait()

    def widen(g, _):
        flat[pl.ds(g * 512, 512), :] = x_ref[pl.ds(g * 16, 16)].astype(F32).reshape(512, 128)
        return 0

    lax.fori_loop(0, CHAN // 16, widen, 0)
    same = lax.broadcasted_iota(jnp.int32, (COLS, COLS), 0) == lax.broadcasted_iota(
        jnp.int32, (COLS, COLS), 1
    )
    unit = same.astype(F32).astype(BF16)

    def turn(t, _):
        for u in range(8):
            i = t * 8 + u
            line = flat[pl.ds(i, CHAN, stride=ROWS), :].astype(BF16)
            both = jnp.concatenate([line, line], axis=0)
            frame[ROW_PAD + i, COL_PAD : COL_PAD + COLS, :] = lax.dot_general(
                unit, both, NT, preferred_element_type=F32
            )
        return 0

    lax.fori_loop(0, ROWS // 8, turn, 0)

    def prepare_one():
        for name in ("1a", "b1a", "1b", "b1b"):
            loads[name].wait()
        for ky in range(3):
            for target, kernel in ((w1a, k1a), (w1b, k1b)):
                taps = three_taps(kernel, ky)
                target[:, ky * 256 : ky * 256 + 256] = jnp.concatenate([taps, taps], axis=0)

    def prepare_two():
        for name in ("2a", "b2a", "2b", "b2b"):
            loads[name].wait()
        zeros = jnp.zeros((CHAN, CHAN), BF16)
        for ky in range(3):
            w2a[:, ky * 256 : ky * 256 + 256] = jnp.concatenate(
                [three_taps(k2a, ky), three_taps(k2a, ky, True)], axis=0
            )
            for kx in range(3):
                upper = jnp.concatenate([k2b[ky, kx], zeros], axis=1)
                lower = jnp.concatenate([zeros, k2b[kx, ky]], axis=1)
                at = ky * 384 + kx * 128
                w2b[:, at : at + 128] = jnp.concatenate([upper, lower], axis=0)

    def bias(ref):
        return jnp.concatenate([ref[...], ref[...]], axis=1)

    def clear_outside():
        @pl.when(row == 0)
        def _():
            hidden[0:HID_ROW] = jnp.zeros((HID_ROW, 144, 128), F32)

        @pl.when(row == 31)
        def _():
            hidden[HID_ROW + ROWS :] = jnp.zeros((HID_ROW, 144, 128), F32)

        @pl.when(col == 0)
        def _():
            hidden[:, 0:HID_COL, :] = jnp.zeros((ROWS + 2 * HID_ROW, HID_COL, 128), F32)

        @pl.when(col == SIDE - 1)
        def _():
            hidden[:, HID_COL + COLS :, :] = jnp.zeros((ROWS + 2 * HID_ROW, HID_COL, 128), F32)

    halo = Halo(4, frame, halo_send.at[0], halo_recv.at[0], halo_ss.at[0], halo_rs.at[0], row, col)
    halo.pack(ORDER)
    pl.semaphore_wait(barrier, waits)
    halo.start()
    prepare_one()

    everywhere, borders = ((0, 144),), ((0, 16), (128, 144))

    def shifted(d, top, spans=everywhere):
        def one(t, _):
            for u in range(4):
                i = top + t * 4 + u
                for low, high in spans:
                    at, many = COL_PAD - HID_COL + low, high - low
                    left = frame[i, at - d : at - d + many, :]
                    here = frame[i, at : at + many, :]
                    right = frame[i, at + d : at + d + many, :]
                    slab[i, low:high, 0:128] = paired(left, here).astype(BF16)
                    slab[i, low:high, 128:256] = right.astype(BF16)
            return 0

        return one

    def conv_a(d, weights, bias_ref, first, step, spans=everywhere):
        def one(t, _):
            i = first + t * step
            for low, high in spans:
                many = high - low
                lhs = jnp.concatenate(
                    [
                        slab[pl.ds(i + ROW_PAD + ky * d, step), low:high, :].reshape(
                            step * many, 256
                        )
                        for ky in (-1, 0, 1)
                    ],
                    axis=1,
                )
                total = lax.dot_general(lhs, weights[...], NT, preferred_element_type=F32)
                value = rounded(elu(total + bias(bias_ref)))
                hidden[pl.ds(i + HID_ROW, step), low:high, :] = value.reshape(step, many, 128)
            return 0

        return one

    full, sides = ((0, 128),), ((0, 16), (112, 128))

    def hidden_taps(first, spans):
        def one(t, _):
            for u in range(4):
                i = first + t * 4 + u
                at = i + HID_ROW
                for low, high in spans:
                    left = hidden[at, HID_COL - 2 + low : HID_COL - 2 + high, :]
                    here = hidden[at, HID_COL + low : HID_COL + high, :]
                    right = hidden[at, HID_COL + 2 + low : HID_COL + 2 + high, :]
                    wide[i + 2, low:high, 0:128] = paired(left, here).astype(BF16)
                    wide[i + 2, low:high, 128:256] = right.astype(BF16)
            return 0

        return one

    def conv_b_one(first, step, spans):
        def one(t, _):
            i = first + t * step
            for low, high in spans:
                many = high - low
                lhs = jnp.concatenate(
                    [
                        wide[pl.ds(i + 2 * ky, step), low:high, 0:256].reshape(step * many, 256)
                        for ky in range(3)
                    ],
                    axis=1,
                )
                total = lax.dot_general(lhs, w1b[...], NT, preferred_element_type=F32)
                here = frame[pl.ds(ROW_PAD + i, step), COL_PAD + low : COL_PAD + high, :]
                value = rounded(elu(here.reshape(step * many, 128) + total + bias(b1b)))
                for u in range(step):
                    at = pl.multiple_of((i + u) * COLS + low, 16)
                    block_y[pl.ds(at, many), :] = value[u * many : (u + 1) * many]
            return 0

        return one

    lax.fori_loop(0, 8, shifted(2, ROW_PAD), 0)
    lax.fori_loop(0, 2, conv_a(2, w1a, b1a, 2, 14), 0)
    lax.fori_loop(0, 7, hidden_taps(2, full), 0)
    lax.fori_loop(0, 2, conv_b_one(4, 12, full), 0)
    halo.finish(SIDEWAYS)
    lax.fori_loop(0, 8, shifted(2, ROW_PAD, borders), 0)
    lax.fori_loop(0, 1, conv_a(2, w1a, b1a, 2, 28, borders), 0)
    halo.finish(OTHERS)
    lax.fori_loop(0, 1, shifted(2, ROW_PAD - 4), 0)
    lax.fori_loop(0, 1, shifted(2, ROW_PAD + 32), 0)
    lax.fori_loop(0, 1, conv_a(2, w1a, b1a, -2, 4), 0)
    lax.fori_loop(0, 1, conv_a(2, w1a, b1a, 30, 4), 0)
    clear_outside()
    lax.fori_loop(0, 1, hidden_taps(-2, full), 0)
    lax.fori_loop(0, 1, hidden_taps(30, full), 0)
    lax.fori_loop(0, 7, hidden_taps(2, sides), 0)
    lax.fori_loop(0, 1, conv_b_one(0, 4, full), 0)
    lax.fori_loop(0, 1, conv_b_one(28, 4, full), 0)
    lax.fori_loop(0, 1, conv_b_one(4, 24, sides), 0)

    def spread(t, _):
        via = nearby(col, t)
        for k in range(QUAD):
            for u in range(4):
                column = block_y[pl.ds(32 * k + 4 * rows_at(t) + u, ROWS, stride=COLS), :]
                outbox[via, k, u] = paired(column[:16], column[16:]).astype(BF16)
            alone = jnp.logical_and(t == 0, quarter == k)

            @pl.when(alone)
            def _():
                pltpu.make_async_copy(
                    outbox.at[via, k], transit.at[col, quarter], rs1.at[col]
                ).start()

            @pl.when(jnp.logical_not(alone))
            def _():
                pltpu.make_async_remote_copy(
                    outbox.at[via, k],
                    transit.at[col, quarter],
                    ss1,
                    rs1.at[col],
                    device_id=(z * QUAD + k, via),
                    device_id_type=MESH,
                ).start()

        return 0

    lax.fori_loop(0, SIDE, spread, 0)

    def forward(t, _):
        origin = nearby(col, t)
        pltpu.make_async_copy(transit.at[origin], transit.at[origin], rs1.at[origin]).wait()
        alone = jnp.logical_and(origin == z, col == z)

        @pl.when(alone)
        def _():
            pltpu.make_async_copy(transit.at[origin], inbox.at[col], rs2.at[col]).start()

        @pl.when(jnp.logical_not(alone))
        def _():
            pltpu.make_async_remote_copy(
                transit.at[origin],
                inbox.at[col],
                ss2,
                rs2.at[col],
                device_id=(origin * QUAD + quarter, z),
                device_id_type=MESH,
            ).start()

        return 0

    lax.fori_loop(0, SIDE, forward, 0)
    prepare_two()

    def arrive(t, _):
        via = nearby(z, t)
        pltpu.make_async_copy(inbox.at[via], inbox.at[via], rs2.at[via]).wait()
        for u in range(4):
            i = rows_at(t) * 4 + u
            for k in range(QUAD):
                mirror = doubled(inbox[via, k, u].astype(F32))
                for half in range(2):
                    j = 32 * k + 16 * half
                    own = block_y[pl.ds(pl.multiple_of(i * COLS + j, 16), 16), :]
                    frame[ROW_PAD + i, COL_PAD + j : COL_PAD + j + 16, :] = rounded(
                        (own + mirror[half]) * 0.5
                    )
        return 0

    halo = Halo(8, frame, halo_send.at[1], halo_recv.at[1], halo_ss.at[1], halo_rs.at[1], row, col)
    lax.fori_loop(0, SIDE // 2, arrive, 0)
    halo.pack(OTHERS, True)
    lax.fori_loop(SIDE // 2, SIDE, arrive, 0)
    halo.pack(SIDEWAYS, True)
    halo.finish(OTHERS)

    lax.fori_loop(0, 12, shifted(4, 0), 0)
    lax.fori_loop(0, 2, conv_a(4, w2a, b2a, -4, 20), 0)
    halo.finish(SIDEWAYS)
    lax.fori_loop(0, 12, shifted(4, 0, borders), 0)
    lax.fori_loop(0, 1, conv_a(4, w2a, b2a, -4, 40, borders), 0)
    clear_outside()

    def wide_taps(t, _):
        for u in range(4):
            i = t * 4 + u
            for kx in range(3):
                at = HID_COL + 4 * (kx - 1)
                wide[i, :, kx * 128 : kx * 128 + 128] = hidden[i, at : at + 128, :].astype(BF16)
        return 0

    lax.fori_loop(0, 10, wide_taps, 0)

    lane = lax.broadcasted_iota(jnp.int32, (CHAN, 128), 1)
    chan = lax.broadcasted_iota(jnp.int32, (CHAN, 128), 0)
    mean = jnp.where(jnp.logical_or(lane == chan, lane == chan + CHAN), 0.5, 0.0).astype(BF16)

    def conv_b_two(t, _):
        i = t * 8
        lhs = jnp.concatenate(
            [wide[pl.ds(i + 4 * ky, 8)].reshape(1024, 384) for ky in range(3)], axis=1
        )
        total = lax.dot_general(lhs, w2b[...], NT, preferred_element_type=F32)
        here = frame[pl.ds(ROW_PAD + i, 8), COL_PAD : COL_PAD + COLS, :].reshape(1024, 128)
        both = elu(here + total + bias(b2b)).astype(BF16)
        for u in range(8):
            line = both[u * COLS : (u + 1) * COLS]
            flat[pl.ds(i + u, CHAN, stride=ROWS), :] = lax.dot_general(
                mean, line, NT, preferred_element_type=F32
            )
        return 0

    lax.fori_loop(0, ROWS // 8, conv_b_two, 0)

    def narrow(g, _):
        out_ref[pl.ds(g * 8, 8)] = flat[pl.ds(g * 256, 256), :].reshape(8, ROWS, COLS).astype(BF16)
        return 0

    lax.fori_loop(0, CHAN // 8, narrow, 0)

    def sent_one(t, _):
        for k in range(QUAD):

            @pl.when(jnp.logical_not(jnp.logical_and(t == 0, quarter == k)))
            def _():
                pltpu.make_async_copy(outbox.at[0, 0], outbox.at[0, 0], ss1).wait()

        @pl.when(jnp.logical_or(t > 0, col != z))
        def _():
            pltpu.make_async_copy(transit.at[0], transit.at[0], ss2).wait()

        return 0

    lax.fori_loop(0, SIDE, sent_one, 0)


def shards(pair_map, k1a, b1a, k1b, b1b, k2a, b2a, k2b, b2b):
    wide = lambda b: b.reshape(1, CHAN)
    vmem = pl.BlockSpec(memory_space=pltpu.VMEM)
    dma, regular = pltpu.SemaphoreType.DMA, pltpu.SemaphoreType.REGULAR
    return pl.pallas_call(
        body,
        out_shape=jax.ShapeDtypeStruct((CHAN, ROWS, COLS), BF16),
        in_specs=[pl.BlockSpec(memory_space=pl.ANY)] * 9,
        out_specs=vmem,
        scratch_shapes=[
            pltpu.VMEM((CHAN, ROWS, COLS), BF16),
            *[pltpu.VMEM((3, 3, CHAN, CHAN), BF16) for _ in range(4)],
            *[pltpu.VMEM((1, CHAN), F32) for _ in range(4)],
            dma((9,)),
            pltpu.VMEM((CHAN * ROWS, COLS), F32),
            pltpu.VMEM((ROWS + 2 * ROW_PAD, COLS + 2 * COL_PAD, 128), F32),
            pltpu.VMEM((ROWS + 2 * ROW_PAD, 144, 256), BF16),
            pltpu.VMEM((ROWS + 2 * HID_ROW, 144, 128), F32),
            pltpu.VMEM((ROWS + 2 * HID_ROW, COLS, 384), BF16),
            pltpu.VMEM((ROWS * COLS, 128), F32),
            pltpu.VMEM((SIDE, QUAD, 4, 16, 128), BF16),
            pltpu.VMEM((SIDE, QUAD, 4, 16, 128), BF16),
            pltpu.VMEM((SIDE, QUAD, 4, 16, 128), BF16),
            pltpu.VMEM((2, 8, 32, 16, 128), BF16),
            pltpu.VMEM((2, 8, 32, 16, 128), BF16),
            pltpu.VMEM((128, 768), BF16),
            pltpu.VMEM((128, 768), BF16),
            pltpu.VMEM((128, 768), BF16),
            pltpu.VMEM((128, 1152), BF16),
            dma((2, 8)),
            dma((2, 8)),
            dma,
            dma((SIDE,)),
            dma,
            dma((SIDE,)),
        ],
        compiler_params=pltpu.CompilerParams(
            collective_id=0, has_side_effects=True, vmem_limit_bytes=50 << 20
        ),
    )(pair_map, k1a, wide(b1a), k1b, wide(b1b), k2a, wide(b2a), k2b, wide(b2b))


def solution(mesh):
    placed = (P(None, "row", "col"), P(), P(), P(), P(), P(), P(), P(), P())
    return jax.shard_map(
        shards, mesh=mesh, in_specs=placed, out_specs=P(None, "row", "col"), check_vma=False
    )
```

```python
import functools

import jax
import jax.numpy as jnp
from jax import lax
from jax.experimental import pallas as pl
from jax.experimental.pallas import tpu as pltpu
from jax.sharding import PartitionSpec as P

MESH = pl.DeviceIdType.MESH
F32, BF16 = jnp.float32, jnp.bfloat16
NT = (((1,), (1,)), ((), ()))
ROWS, COLS, CHAN, SIDE, QUAD = 32, 128, 64, 8, 4
ROW_PAD, COL_PAD, HID_ROW, HID_COL = 8, 16, 4, 8
NEIGHBOURS = [(-1, 0), (-1, -1), (-1, 1), (0, -1), (0, 1), (1, -1), (1, 1), (1, 0)]
ORDER = [0, 7, 1, 2, 5, 6, 3, 4]
SIDEWAYS, OTHERS = [3, 4], [0, 7, 1, 2, 5, 6]


def elu(v):
    return jnp.where(v > 0, v, jnp.exp(jnp.minimum(v, 0.0)) - 1.0)


def rounded(v):
    return v.astype(BF16).astype(F32)


def low_lanes(shape):
    return lax.broadcasted_iota(jnp.int32, shape, len(shape) - 1) < CHAN


def doubled(packed):
    turned = pltpu.roll(packed, CHAN, packed.ndim - 1)
    low = low_lanes(packed.shape)
    return jnp.where(low, packed, turned), jnp.where(low, turned, packed)


def paired(first, second):
    return jnp.where(low_lanes(first.shape), first, second)


def nearby(at, step):
    upper = step // 4
    middle = lax.rem(upper + step // 2, 2)
    return (
        lax.rem(at // 4 + upper, 2) * 4
        + lax.rem(at // 2 + middle, 2) * 2
        + lax.rem(at + step, 2)
    )


def rows_at(step):
    return 2 * lax.rem(3 * (step // 2), 4) + lax.rem(step, 2)


class Halo:
    def __init__(self, rows, frame, send, recv, send_sem, recv_sem, row, col):
        self.rows, self.frame = rows, frame
        self.send, self.recv = send, recv
        self.send_sem, self.recv_sem = send_sem, recv_sem
        self.row, self.col = row, col

    def parts(self, at):
        dr, dc = NEIGHBOURS[at]
        if dc == 0:
            return 0 if dr < 0 else 1, self.rows * 4
        if dr == 0:
            return 2 if dc < 0 else 3, 8
        return 4 + (dr > 0) * 2 + (dc > 0), self.rows // 4

    def copy(self, at):
        dr, dc = NEIGHBOURS[at]
        there = len(NEIGHBOURS) - 1 - at
        mine, count = self.parts(at)
        other, _ = self.parts(there)
        device = (lax.rem(self.row + dr + 32, 32), lax.rem(self.col + dc + SIDE, SIDE))
        return pltpu.make_async_remote_copy(
            self.send.at[mine, pl.ds(0, count)],
            self.recv.at[other, pl.ds(0, count)],
            self.send_sem.at[mine],
            self.recv_sem.at[other],
            device_id=device,
            device_id_type=MESH,
        )

    def incoming(self, at):
        mine, count = self.parts(at)
        there = self.recv.at[mine, pl.ds(0, count)]
        return pltpu.make_async_copy(there, there, self.recv_sem.at[mine])

    def pack(self, which, start=False):
        frame, rows = self.frame, self.rows
        for at in which:
            dr, dc = NEIGHBOURS[at]
            mine, _ = self.parts(at)
            top = ROW_PAD if dr < 0 else ROW_PAD + ROWS - rows
            left = COL_PAD if dc < 0 else COL_PAD + COLS - 8
            if dc == 0:

                lines = frame[top : top + rows, COL_PAD : COL_PAD + COLS, :]
                both = paired(lines[:, :64], lines[:, 64:]).astype(BF16)
                self.send[mine, 0 : rows * 4] = both.reshape(rows * 4, 16, 128)
            else:
                base, many = (ROW_PAD, ROWS // 4) if dr == 0 else (top, rows // 4)

                for t in range(many):
                    block = frame[base + 4 * t : base + 4 * t + 4, left : left + 8, :]
                    both = paired(block[:2].reshape(16, 128), block[2:].reshape(16, 128))
                    self.send[mine, t] = both.astype(BF16)
            if start:
                self.copy(at).start()

    def start(self):
        for at in ORDER:
            self.copy(at).start()

    def finish(self, which):
        frame, rows = self.frame, self.rows
        for at in which:
            dr, dc = NEIGHBOURS[at]
            self.incoming(at).wait()
            mine, _ = self.parts(at)
            inside = jnp.logical_and(
                jnp.logical_and(self.row + dr >= 0, self.row + dr < 32),
                jnp.logical_and(self.col + dc >= 0, self.col + dc < SIDE),
            )
            top = ROW_PAD - rows if dr < 0 else ROW_PAD + ROWS
            left = COL_PAD - 8 if dc < 0 else COL_PAD + COLS
            if dc == 0:

                for i in range(rows):
                    line = self.recv[mine, i * 4 : i * 4 + 4].reshape(64, 128).astype(F32)
                    first, second = doubled(jnp.where(inside, line, 0.0))
                    frame[top + i, COL_PAD : COL_PAD + 64, :] = first
                    frame[top + i, COL_PAD + 64 : COL_PAD + 128, :] = second
            else:
                base, many = (ROW_PAD, ROWS // 4) if dr == 0 else (top, rows // 4)

                for t in range(many):
                    block = self.recv[mine, t].astype(F32)
                    first, second = doubled(jnp.where(inside, block, 0.0))
                    i = base + 4 * t
                    frame[i : i + 2, left : left + 8, :] = first.reshape(2, 8, 128)
                    frame[i + 2 : i + 4, left : left + 8, :] = second.reshape(2, 8, 128)
        for at in which:
            self.copy(at).wait_send()


def three_taps(kernel, ky, swapped=False):
    pick = lambda kx: kernel[kx, ky] if swapped else kernel[ky, kx]
    zeros = jnp.zeros((CHAN, CHAN), BF16)
    return jnp.concatenate([pick(0), pick(1), pick(2), zeros], axis=1)


def body(
    x_hbm, k1a_hbm, b1a_hbm, k1b_hbm, b1b_hbm, k2a_hbm, b2a_hbm, k2b_hbm, b2b_hbm, out_ref,
    x_ref, k1a, k1b, k2a, k2b, b1a, b1b, b2a, b2b, load_sem, flat, frame, slab, hidden, wide, block_y, outbox, transit, inbox,
    halo_send, halo_recv, w1a, w1b, w2a, w2b,
    halo_ss, halo_rs, ss1, rs1, ss2, rs2,
):
    row, col = lax.axis_index("row"), lax.axis_index("col")
    z, quarter = row // QUAD, lax.rem(row, QUAD)

    loads = {"x": pltpu.make_async_copy(x_hbm, x_ref, load_sem.at[0])}
    loads["x"].start()

    barrier = pltpu.get_barrier_semaphore()

    def greet(device):
        pl.semaphore_signal(barrier, inc=1, device_id=device, device_id_type=MESH)

    for dr, dc in NEIGHBOURS:
        greet((lax.rem(row + dr + 32, 32), lax.rem(col + dc + SIDE, SIDE)))

    def greet_plane(t, _):
        other = lax.rem(col + t, SIDE)
        for k in range(QUAD):

            @pl.when(jnp.logical_or(t > 0, quarter != k))
            def _():
                greet((z * QUAD + k, other))

        @pl.when(jnp.logical_or(col != z, t > 0))
        def _():
            greet((col * QUAD + quarter, other))

        return 0

    lax.fori_loop(0, SIDE, greet_plane, 0)
    waits = 8 + 31 + SIDE - jnp.where(col == z, 1, 0)

    for at, (name, source, target) in enumerate(
        (
            ("1a", k1a_hbm, k1a), ("b1a", b1a_hbm, b1a),
            ("1b", k1b_hbm, k1b), ("b1b", b1b_hbm, b1b), ("2a", k2a_hbm, k2a),
            ("b2a", b2a_hbm, b2a), ("2b", k2b_hbm, k2b), ("b2b", b2b_hbm, b2b),
        )
    ):
        loads[name] = pltpu.make_async_copy(source, target, load_sem.at[at + 1])
        loads[name].start()

    loads["x"].wait()

    def widen(g, _):
        flat[pl.ds(g * 512, 512), :] = x_ref[pl.ds(g * 16, 16)].astype(F32).reshape(512, 128)
        return 0

    lax.fori_loop(0, CHAN // 16, widen, 0)
    same = lax.broadcasted_iota(jnp.int32, (COLS, COLS), 0) == lax.broadcasted_iota(
        jnp.int32, (COLS, COLS), 1
    )
    unit = same.astype(F32).astype(BF16)

    def turn(t, _):
        for u in range(8):
            i = t * 8 + u
            line = flat[pl.ds(i, CHAN, stride=ROWS), :].astype(BF16)
            both = jnp.concatenate([line, line], axis=0)
            frame[ROW_PAD + i, COL_PAD : COL_PAD + COLS, :] = lax.dot_general(
                unit, both, NT, preferred_element_type=F32
            )
        return 0

    lax.fori_loop(0, ROWS // 8, turn, 0)

    def prepare_one():
        for name in ("1a", "b1a", "1b", "b1b"):
            loads[name].wait()
        for ky in range(3):
            for target, kernel in ((w1a, k1a), (w1b, k1b)):
                taps = three_taps(kernel, ky)
                target[:, ky * 256 : ky * 256 + 256] = jnp.concatenate([taps, taps], axis=0)

    def prepare_two():
        for name in ("2a", "b2a", "2b", "b2b"):
            loads[name].wait()
        zeros = jnp.zeros((CHAN, CHAN), BF16)
        for ky in range(3):
            w2a[:, ky * 256 : ky * 256 + 256] = jnp.concatenate(
                [three_taps(k2a, ky), three_taps(k2a, ky, True)], axis=0
            )
            for kx in range(3):
                upper = jnp.concatenate([k2b[ky, kx], zeros], axis=1)
                lower = jnp.concatenate([zeros, k2b[kx, ky]], axis=1)
                at = ky * 384 + kx * 128
                w2b[:, at : at + 128] = jnp.concatenate([upper, lower], axis=0)

    def bias(ref):
        return jnp.concatenate([ref[...], ref[...]], axis=1)

    def clear_outside():
        @pl.when(row == 0)
        def _():
            hidden[0:HID_ROW] = jnp.zeros((HID_ROW, 144, 128), F32)

        @pl.when(row == 31)
        def _():
            hidden[HID_ROW + ROWS :] = jnp.zeros((HID_ROW, 144, 128), F32)

        @pl.when(col == 0)
        def _():
            hidden[:, 0:HID_COL, :] = jnp.zeros((ROWS + 2 * HID_ROW, HID_COL, 128), F32)

        @pl.when(col == SIDE - 1)
        def _():
            hidden[:, HID_COL + COLS :, :] = jnp.zeros((ROWS + 2 * HID_ROW, HID_COL, 128), F32)

    halo = Halo(4, frame, halo_send.at[0], halo_recv.at[0], halo_ss.at[0], halo_rs.at[0], row, col)
    halo.pack(ORDER)
    prepare_one()
    pl.semaphore_wait(barrier, waits)
    halo.start()

    everywhere, borders = ((0, 144),), ((0, 16), (128, 144))

    def shifted(d, top, spans=everywhere):
        def one(t, _):
            for u in range(4):
                i = top + t * 4 + u
                for low, high in spans:
                    at, many = COL_PAD - HID_COL + low, high - low
                    left = frame[i, at - d : at - d + many, :]
                    here = frame[i, at : at + many, :]
                    right = frame[i, at + d : at + d + many, :]
                    slab[i, low:high, 0:128] = paired(left, here).astype(BF16)
                    slab[i, low:high, 128:256] = right.astype(BF16)
            return 0

        return one

    def conv_a(d, weights, bias_ref, first, step, spans=everywhere):
        def one(t, _):
            i = first + t * step
            for low, high in spans:
                many = high - low
                lhs = jnp.concatenate(
                    [
                        slab[pl.ds(i + ROW_PAD + ky * d, step), low:high, :].reshape(
                            step * many, 256
                        )
                        for ky in (-1, 0, 1)
                    ],
                    axis=1,
                )
                total = lax.dot_general(lhs, weights[...], NT, preferred_element_type=F32)
                value = rounded(elu(total + bias(bias_ref)))
                hidden[pl.ds(i + HID_ROW, step), low:high, :] = value.reshape(step, many, 128)
            return 0

        return one

    full, sides = ((0, 128),), ((0, 16), (112, 128))

    def hidden_taps(first, spans):
        def one(t, _):
            for u in range(4):
                i = first + t * 4 + u
                at = i + HID_ROW
                for low, high in spans:
                    left = hidden[at, HID_COL - 2 + low : HID_COL - 2 + high, :]
                    here = hidden[at, HID_COL + low : HID_COL + high, :]
                    right = hidden[at, HID_COL + 2 + low : HID_COL + 2 + high, :]
                    wide[i + 2, low:high, 0:128] = paired(left, here).astype(BF16)
                    wide[i + 2, low:high, 128:256] = right.astype(BF16)
            return 0

        return one

    def conv_b_one(first, step, spans):
        def one(t, _):
            i = first + t * step
            for low, high in spans:
                many = high - low
                lhs = jnp.concatenate(
                    [
                        wide[pl.ds(i + 2 * ky, step), low:high, 0:256].reshape(step * many, 256)
                        for ky in range(3)
                    ],
                    axis=1,
                )
                total = lax.dot_general(lhs, w1b[...], NT, preferred_element_type=F32)
                here = frame[pl.ds(ROW_PAD + i, step), COL_PAD + low : COL_PAD + high, :]
                value = rounded(elu(here.reshape(step * many, 128) + total + bias(b1b)))
                for u in range(step):
                    at = pl.multiple_of((i + u) * COLS + low, 16)
                    block_y[pl.ds(at, many), :] = value[u * many : (u + 1) * many]
            return 0

        return one

    lax.fori_loop(0, 8, shifted(2, ROW_PAD), 0)
    lax.fori_loop(0, 2, conv_a(2, w1a, b1a, 2, 14), 0)
    lax.fori_loop(0, 7, hidden_taps(2, full), 0)
    lax.fori_loop(0, 2, conv_b_one(4, 12, full), 0)
    halo.finish(SIDEWAYS)
    lax.fori_loop(0, 8, shifted(2, ROW_PAD, borders), 0)
    lax.fori_loop(0, 1, conv_a(2, w1a, b1a, 2, 28, borders), 0)
    halo.finish(OTHERS)
    lax.fori_loop(0, 1, shifted(2, ROW_PAD - 4), 0)
    lax.fori_loop(0, 1, shifted(2, ROW_PAD + 32), 0)
    lax.fori_loop(0, 1, conv_a(2, w1a, b1a, -2, 4), 0)
    lax.fori_loop(0, 1, conv_a(2, w1a, b1a, 30, 4), 0)
    clear_outside()
    lax.fori_loop(0, 1, hidden_taps(-2, full), 0)
    lax.fori_loop(0, 1, hidden_taps(30, full), 0)
    lax.fori_loop(0, 7, hidden_taps(2, sides), 0)
    lax.fori_loop(0, 1, conv_b_one(0, 4, full), 0)
    lax.fori_loop(0, 1, conv_b_one(28, 4, full), 0)
    lax.fori_loop(0, 1, conv_b_one(4, 24, sides), 0)

    def spread(t, _):
        via = nearby(col, t)
        for k in range(QUAD):
            for u in range(4):
                column = block_y[pl.ds(32 * k + 4 * rows_at(t) + u, ROWS, stride=COLS), :]
                outbox[via, k, u] = paired(column[:16], column[16:]).astype(BF16)
            alone = jnp.logical_and(t == 0, quarter == k)

            @pl.when(alone)
            def _():
                pltpu.make_async_copy(
                    outbox.at[via, k], transit.at[col, quarter], rs1.at[col]
                ).start()

            @pl.when(jnp.logical_not(alone))
            def _():
                pltpu.make_async_remote_copy(
                    outbox.at[via, k],
                    transit.at[col, quarter],
                    ss1,
                    rs1.at[col],
                    device_id=(z * QUAD + k, via),
                    device_id_type=MESH,
                ).start()

        return 0

    lax.fori_loop(0, SIDE, spread, 0)

    def forward(t, _):
        origin = nearby(col, t)
        pltpu.make_async_copy(transit.at[origin], transit.at[origin], rs1.at[origin]).wait()
        alone = jnp.logical_and(origin == z, col == z)

        @pl.when(alone)
        def _():
            pltpu.make_async_copy(transit.at[origin], inbox.at[col], rs2.at[col]).start()

        @pl.when(jnp.logical_not(alone))
        def _():
            pltpu.make_async_remote_copy(
                transit.at[origin],
                inbox.at[col],
                ss2,
                rs2.at[col],
                device_id=(origin * QUAD + quarter, z),
                device_id_type=MESH,
            ).start()

        return 0

    lax.fori_loop(0, SIDE, forward, 0)
    prepare_two()

    def arrive(t, _):
        via = nearby(z, t)
        pltpu.make_async_copy(inbox.at[via], inbox.at[via], rs2.at[via]).wait()
        for u in range(4):
            i = rows_at(t) * 4 + u
            for k in range(QUAD):
                mirror = doubled(inbox[via, k, u].astype(F32))
                for half in range(2):
                    j = 32 * k + 16 * half
                    own = block_y[pl.ds(pl.multiple_of(i * COLS + j, 16), 16), :]
                    frame[ROW_PAD + i, COL_PAD + j : COL_PAD + j + 16, :] = rounded(
                        (own + mirror[half]) * 0.5
                    )
        shifted(4, ROW_PAD)(rows_at(t), 0)
        return 0

    halo = Halo(8, frame, halo_send.at[1], halo_recv.at[1], halo_ss.at[1], halo_rs.at[1], row, col)
    lax.fori_loop(0, SIDE // 2, arrive, 0)
    halo.pack(OTHERS, True)
    lax.fori_loop(SIDE // 2, SIDE, arrive, 0)
    halo.pack(SIDEWAYS, True)
    lax.fori_loop(0, 2, conv_a(4, w2a, b2a, 4, 12), 0)
    halo.finish(OTHERS)
    lax.fori_loop(0, 2, shifted(4, 0), 0)
    lax.fori_loop(0, 2, shifted(4, ROW_PAD + 32), 0)
    lax.fori_loop(0, 1, conv_a(4, w2a, b2a, -4, 8), 0)
    lax.fori_loop(0, 1, conv_a(4, w2a, b2a, 28, 8), 0)
    halo.finish(SIDEWAYS)
    lax.fori_loop(0, 12, shifted(4, 0, borders), 0)
    lax.fori_loop(0, 1, conv_a(4, w2a, b2a, -4, 40, borders), 0)
    clear_outside()

    def wide_taps(t, _):
        for u in range(4):
            i = t * 4 + u
            for kx in range(3):
                at = HID_COL + 4 * (kx - 1)
                wide[i, :, kx * 128 : kx * 128 + 128] = hidden[i, at : at + 128, :].astype(BF16)
        return 0

    lax.fori_loop(0, 10, wide_taps, 0)

    lane = lax.broadcasted_iota(jnp.int32, (CHAN, 128), 1)
    chan = lax.broadcasted_iota(jnp.int32, (CHAN, 128), 0)
    mean = jnp.where(jnp.logical_or(lane == chan, lane == chan + CHAN), 0.5, 0.0).astype(BF16)

    def conv_b_two(t, _):
        i = t * 8
        lhs = jnp.concatenate(
            [wide[pl.ds(i + 4 * ky, 8)].reshape(1024, 384) for ky in range(3)], axis=1
        )
        total = lax.dot_general(lhs, w2b[...], NT, preferred_element_type=F32)
        here = frame[pl.ds(ROW_PAD + i, 8), COL_PAD : COL_PAD + COLS, :].reshape(1024, 128)
        both = elu(here + total + bias(b2b)).astype(BF16)
        for u in range(8):
            line = both[u * COLS : (u + 1) * COLS]
            flat[pl.ds(i + u, CHAN, stride=ROWS), :] = lax.dot_general(
                mean, line, NT, preferred_element_type=F32
            )
        return 0

    lax.fori_loop(0, ROWS // 8, conv_b_two, 0)

    def narrow(g, _):
        out_ref[pl.ds(g * 8, 8)] = flat[pl.ds(g * 256, 256), :].reshape(8, ROWS, COLS).astype(BF16)
        return 0

    lax.fori_loop(0, CHAN // 8, narrow, 0)

    def sent_one(t, _):
        for k in range(QUAD):

            @pl.when(jnp.logical_not(jnp.logical_and(t == 0, quarter == k)))
            def _():
                pltpu.make_async_copy(outbox.at[0, 0], outbox.at[0, 0], ss1).wait()

        @pl.when(jnp.logical_or(t > 0, col != z))
        def _():
            pltpu.make_async_copy(transit.at[0], transit.at[0], ss2).wait()

        return 0

    lax.fori_loop(0, SIDE, sent_one, 0)


def shards(pair_map, k1a, b1a, k1b, b1b, k2a, b2a, k2b, b2b):
    wide = lambda b: b.reshape(1, CHAN)
    vmem = pl.BlockSpec(memory_space=pltpu.VMEM)
    dma, regular = pltpu.SemaphoreType.DMA, pltpu.SemaphoreType.REGULAR
    return pl.pallas_call(
        body,
        out_shape=jax.ShapeDtypeStruct((CHAN, ROWS, COLS), BF16),
        in_specs=[pl.BlockSpec(memory_space=pl.ANY)] * 9,
        out_specs=vmem,
        scratch_shapes=[
            pltpu.VMEM((CHAN, ROWS, COLS), BF16),
            *[pltpu.VMEM((3, 3, CHAN, CHAN), BF16) for _ in range(4)],
            *[pltpu.VMEM((1, CHAN), F32) for _ in range(4)],
            dma((9,)),
            pltpu.VMEM((CHAN * ROWS, COLS), F32),
            pltpu.VMEM((ROWS + 2 * ROW_PAD, COLS + 2 * COL_PAD, 128), F32),
            pltpu.VMEM((ROWS + 2 * ROW_PAD, 144, 256), BF16),
            pltpu.VMEM((ROWS + 2 * HID_ROW, 144, 128), F32),
            pltpu.VMEM((ROWS + 2 * HID_ROW, COLS, 384), BF16),
            pltpu.VMEM((ROWS * COLS, 128), F32),
            pltpu.VMEM((SIDE, QUAD, 4, 16, 128), BF16),
            pltpu.VMEM((SIDE, QUAD, 4, 16, 128), BF16),
            pltpu.VMEM((SIDE, QUAD, 4, 16, 128), BF16),
            pltpu.VMEM((2, 8, 32, 16, 128), BF16),
            pltpu.VMEM((2, 8, 32, 16, 128), BF16),
            pltpu.VMEM((128, 768), BF16),
            pltpu.VMEM((128, 768), BF16),
            pltpu.VMEM((128, 768), BF16),
            pltpu.VMEM((128, 1152), BF16),
            dma((2, 8)),
            dma((2, 8)),
            dma,
            dma((SIDE,)),
            dma,
            dma((SIDE,)),
        ],
        compiler_params=pltpu.CompilerParams(
            collective_id=0, has_side_effects=True, vmem_limit_bytes=50 << 20
        ),
    )(pair_map, k1a, wide(b1a), k1b, wide(b1b), k2a, wide(b2a), k2b, wide(b2b))


def solution(mesh):
    placed = (P(None, "row", "col"), P(), P(), P(), P(), P(), P(), P(), P())
    return jax.shard_map(
        shards, mesh=mesh, in_specs=placed, out_specs=P(None, "row", "col"), check_vma=False
    )
```
